32 devices in a mesh: tile: 8 (over y, x, core), slab: 4 (over z).
Axes of the slice: x: 2, y: 2, z: 4, core: 2. Of those that a mesh axis runs over, the one named last changes fastest.
Arguments:
- intensities: bfloat16 [448, 256, 256], P(('tile', 'slab')), may hold values from 0 to 0.5
- object_field: float32 [2, 2, 2048, 384], P(None, None, ('tile', 'slab')), may hold values from -3 to 3
- probe_wave: float32 [256, 512], replicated, may hold values from -6 to 6
- owner_tile: int32 [448], replicated, may hold values from 0 to 7, as said below
- row_offset: int32 [448], replicated, may hold values from 0 to 255
- col_offset: int32 [448], replicated, may hold values from 0 to 1
Outputs:
- gradient: float32 [2, 2, 2048, 384], P(None, None, ('tile', 'slab'))
The draws below stay inside these ranges and needn't reach their ends.
Inputs may be any that keep to these rules, and one draw needn't show every extreme that they name: `owner_tile`: read row r is read by device r // 14 of the tile+slab order. Among the 8 devices of one slab index, the rows of one device name one tile at most 2 times, and each tile is named by at most 16 of their rows; some tile reaches 16 and some device reaches 2 for some tile, for every slab index.
All inputs are finite; a program needn't handle non-finite values.
Results may differ from the reference program's by a relative error of at most 0.006.
The reference program's roundings to bfloat16 on the way count: a program that leaves them out, or rounds other values in their place, can miss the bound.
Values may be sent and summed in bfloat16 or wider, within the bound.
No kernel may reach another device: no remote copies, remote signals or barrier semaphores. Data moves between devices by JAX's collectives and lax.ppermute only.
A program may use at most 64 MiB of HBM per device.

```python
import math
import jax
import jax.numpy as jnp
from jax import lax

PAT = 256
SLICES = 2
TH = 256
OW = 384
COL_STEP = 128
RD = 14
K = 16
ROWS = 2048
READS = 448
N_TILE = 8
N_SLAB = 4


def column_owners(key):
    first_count = K // N_TILE
    keys = jax.random.split(key, 4)
    busiest = jax.random.randint(keys[0], (), 0, N_TILE).astype(jnp.int32)
    relabel = jax.random.permutation(keys[1], N_TILE).astype(jnp.int32)
    others = jax.random.permutation(keys[2], N_TILE - 1).astype(jnp.int32)
    position = jnp.arange(RD, dtype=jnp.int32)[None, :]
    later = jnp.maximum(position - first_count, 0)
    residue = (relabel[:, None] + later // 2) % (N_TILE - 1)
    other_tile = others[residue]
    other_tile = other_tile + (other_tile >= busiest).astype(jnp.int32)
    tile_holders = jnp.where(position < first_count, busiest, other_tile)
    shuffles = jax.vmap(lambda one_key: jax.random.permutation(one_key, RD).astype(jnp.int32))(jax.random.split(keys[3], N_TILE))
    return jnp.take_along_axis(tile_holders, shuffles, 1)


def draw_owner_tile(key, part):
    keys = jax.random.split(jax.random.fold_in(key, 17), N_SLAB)
    owner_table = jax.vmap(column_owners)(keys)
    return jnp.transpose(owner_table, (1, 0, 2)).reshape(-1).astype(jnp.int32)


def touch_ends(entries, rng, least, largest):
    shape = entries.shape
    spot = [jax.random.randint(jax.random.fold_in(rng, axis), (), 0, shape[axis]) for axis in range(len(shape))]
    entries = entries.at[tuple(spot)].set(least)
    longest = shape.index(max(shape))
    spot[longest] = (spot[longest] + 1) % shape[longest]
    return entries.at[tuple(spot)].set(largest)


def block_scale(key, shape, cuts, smallest, high):
    gain, own = 1.0, jax.random.fold_in(key, 6)
    for dim, shards_of in cuts:
        steps = jnp.exp(jax.random.uniform(jax.random.fold_in(own, dim), (shards_of,), jnp.float32, smallest / len(cuts), high / len(cuts)))
        gain = gain * jnp.repeat(steps, shape[dim] // shards_of).reshape([-1 if axis == dim else 1 for axis in range(len(shape))])
    return gain


def noise(rng, shape, width, bound, cuts=(), kind=jnp.bfloat16):
    values = width * jax.random.normal(rng, shape, jnp.float32)
    if cuts:
        values = values * block_scale(rng, shape, cuts, -0.22, 0.18)
    return jnp.clip(values, -bound, bound).astype(kind)


def setup_inputs(seed: int = 0) -> dict:
    seeds = jax.random.split(jax.random.key(seed), 7)
    return {
        "intensities": jnp.clip(0.5 * jax.random.uniform(seeds[0], (READS, PAT, PAT), jnp.float32) ** block_scale(seeds[0], (READS, PAT, PAT), ((0, 32),), -0.2, 0.2), 0.0, 0.5).astype(jnp.bfloat16),
        "object_field": noise(seeds[1], (SLICES, 2, ROWS, OW), 0.5, 3.0, ((2, 32),), jnp.float32),
        "probe_wave": noise(seeds[2], (PAT, 2 * PAT), 1.0, 6.0, (), jnp.float32),
        "owner_tile": draw_owner_tile(jax.random.fold_in(seeds[6], 71), 0),
        "row_offset": touch_ends(jax.random.randint(seeds[4], (READS,), 0, TH), jax.random.fold_in(seeds[4], 1), 0, TH - 1).astype(jnp.int32),
        "col_offset": touch_ends(jax.random.randint(seeds[5], (READS,), 0, (OW - PAT) // COL_STEP + 1), jax.random.fold_in(seeds[5], 1), 0, ((OW - PAT) // COL_STEP + 1) - 1).astype(jnp.int32),
    }


chirp_strength = 40.0

def make_tables(extent):
    counter = jnp.arange(extent, dtype=jnp.int32)
    product_index = counter[:, None] * counter[None, :] % extent
    angles = product_index.astype(jnp.float32) * (2.0 * math.pi / extent)
    scaling = 1.0 / math.sqrt(extent)
    cosine = (jnp.cos(angles) * scaling).astype(jnp.bfloat16)
    sine_part = (jnp.sin(angles) * scaling).astype(jnp.bfloat16)
    forward = jnp.concatenate([jnp.concatenate([cosine, -sine_part], 1), jnp.concatenate([sine_part, cosine], 1)], 0)
    inverse = jnp.concatenate([jnp.concatenate([cosine, sine_part], 1), jnp.concatenate([-sine_part, cosine], 1)], 0)
    frequency = ((counter + extent // 2) % extent - extent // 2).astype(jnp.float32) / extent
    phases = chirp_strength * (frequency[:, None] ** 2 + frequency[None, :] ** 2)
    kernel = jnp.concatenate([jnp.cos(phases), -jnp.sin(phases)], 1)
    return (cosine, sine_part, forward, inverse, kernel)

def transform(field, tables, backward):
    cosine, sine_part, forward, inverse, kernel = tables
    extent = cosine.shape[0]
    halfway = jnp.dot(field, inverse if backward else forward, preferred_element_type=jnp.float32).astype(jnp.bfloat16)
    with_cosine = jnp.dot(cosine, halfway, preferred_element_type=jnp.float32)
    with_sine = jnp.dot(sine_part, halfway, preferred_element_type=jnp.float32)
    if backward:
        real_part = with_cosine[:, :extent] - with_sine[:, extent:]
        imag_part = with_cosine[:, extent:] + with_sine[:, :extent]
    else:
        real_part = with_cosine[:, :extent] + with_sine[:, extent:]
        imag_part = with_cosine[:, extent:] - with_sine[:, :extent]
    return jnp.concatenate([real_part, imag_part], 1)

def complex_product(left, right, conjugate):
    extent = left.shape[1] // 2
    left_real = left[:, :extent]
    left_imag = -left[:, extent:] if conjugate else left[:, extent:]
    right_real = right[:, :extent]
    right_imag = right[:, extent:]
    return jnp.concatenate([left_real * right_real - left_imag * right_imag, left_real * right_imag + left_imag * right_real], 1)

def position_gradient(window, probe_wave, measured, tables):
    kernel = tables[4]
    extent = measured.shape[0]
    layers = window.shape[0]
    pieces = [jnp.concatenate([window[slice_index, 0], window[slice_index, 1]], 1) for slice_index in range(layers)]
    incoming = [probe_wave]
    entering = complex_product(probe_wave, pieces[0], False).astype(jnp.bfloat16)
    for slice_index in range(1, layers):
        spread_wave = complex_product(kernel, transform(entering, tables, False), False).astype(jnp.bfloat16)
        arrived = transform(spread_wave, tables, True)
        incoming.append(arrived)
        entering = complex_product(arrived, pieces[slice_index], False).astype(jnp.bfloat16)
    farfield = transform(entering, tables, False)
    modelled = farfield[:, :extent] ** 2 + farfield[:, extent:] ** 2
    misfit = modelled - measured.astype(jnp.float32)
    far_grad = (farfield * jnp.concatenate([misfit, misfit], 1)).astype(jnp.bfloat16)
    exit_grad = transform(far_grad, tables, True)
    slice_terms = [None] * layers
    for slice_index in range(layers - 1, -1, -1):
        slice_terms[slice_index] = complex_product(incoming[slice_index], exit_grad, True)
        if slice_index > 0:
            back_wave = complex_product(pieces[slice_index], exit_grad, True).astype(jnp.bfloat16)
            back_spread = complex_product(kernel, transform(back_wave, tables, False), True).astype(jnp.bfloat16)
            exit_grad = transform(back_spread, tables, True)
    return jnp.stack([jnp.stack([one_term[:, :extent], one_term[:, extent:]]) for one_term in slice_terms])

def reference(intensities, object_field, probe_wave, owner_tile, row_offset, col_offset):
    extent = intensities.shape[1]
    depth = object_field.shape[0]
    total_rows = object_field.shape[2]
    columns_all = object_field.shape[3]
    tables = make_tables(extent)
    extended = jnp.concatenate([object_field, object_field[:, :, :extent]], 2)

    def accumulate(totals, inputs):
        measured, owner, row_part, col_part = inputs
        top_row = (owner * TH + row_part).astype(jnp.int32)
        left_col = (col_part * COL_STEP).astype(jnp.int32)
        zero_index = jnp.zeros((), jnp.int32)
        starting = (zero_index, zero_index, top_row, left_col)
        window = lax.dynamic_slice(extended, starting, (depth, 2, extent, extent))
        gradient_part = position_gradient(window, probe_wave, measured, tables)
        current = lax.dynamic_slice(totals, starting, (depth, 2, extent, extent))
        return (lax.dynamic_update_slice(totals, current + gradient_part, starting), None)
    initial = jnp.zeros((depth, 2, total_rows + extent, columns_all), jnp.float32)
    totals = lax.scan(accumulate, initial, (intensities, owner_tile, row_offset, col_offset))[0]
    folded = jnp.concatenate([totals[:, :, total_rows:], jnp.zeros((depth, 2, total_rows - extent, columns_all), jnp.float32)], 2)
    return totals[:, :, :total_rows] + folded
```

```python
import functools
import math

import jax
import jax.numpy as jnp
import ml_dtypes
import numpy as np
from jax import lax
from jax.experimental import pallas as pl
from jax.experimental.pallas import tpu as pltpu
from jax.sharding import PartitionSpec as P

K = 16
CAP = 2
COLS = 128
chirp_strength = 40.0
bf16 = jnp.bfloat16
f32 = jnp.float32


def make_tables(extent):
    counter = np.arange(extent, dtype=np.int64)
    angles = (counter[:, None] * counter[None, :] % extent).astype(np.float32) * np.float32(
        2.0 * math.pi / extent
    )
    scaling = np.float32(1.0 / math.sqrt(extent))
    cosine = (np.cos(angles) * scaling).astype(ml_dtypes.bfloat16)
    sine_part = (np.sin(angles) * scaling).astype(ml_dtypes.bfloat16)
    half = extent // 2
    tables = []
    for parity in (0, 1):
        c, s = cosine[:half, parity::2], sine_part[:half, parity::2]
        table = np.concatenate([np.concatenate([c, -s], 1), np.concatenate([s, c], 1)], 0)
        tables += [table, np.ascontiguousarray(table.T)]
    order = np.concatenate([counter[0::2], counter[1::2]])
    frequency = (((counter + half) % extent - half).astype(np.float32) / extent)[order]
    phases = np.float32(chirp_strength) * (frequency[:, None] ** 2 + frequency[None, :] ** 2)
    kernel = np.stack([np.cos(phases), -np.sin(phases)]).astype(np.float32)
    permute = (counter[:, None] == order[None, :]).astype(ml_dtypes.bfloat16)
    return [jnp.asarray(t) for t in tables], jnp.asarray(kernel), jnp.asarray(permute)


def dot(a, b):
    return jnp.dot(a, b, preferred_element_type=f32)


def quads(a, b, h):
    return jnp.concatenate(
        [
            jnp.concatenate([a[:, :h], b[:, :h]], 1),
            jnp.concatenate([a[:, h:], b[:, h:]], 1),
        ],
        0,
    )


def forward(items, tabs):
    a_even, t_even, a_odd, t_odd = tabs
    h = a_even.shape[0] // 2
    sums = [jnp.concatenate([l[0] + r[0], l[1] + r[1]], 1).astype(bf16) for l, r in items]
    diffs = [jnp.concatenate([l[0] - r[0], l[1] - r[1]], 1).astype(bf16) for l, r in items]
    even = [dot(x, a_even) for x in sums]
    odd = [dot(x, a_odd) for x in diffs]
    plus = [quads(a[:h] + a[h:], b[:h] + b[h:], h).astype(bf16) for a, b in zip(even, odd)]
    minus = [quads(a[:h] - a[h:], b[:h] - b[h:], h).astype(bf16) for a, b in zip(even, odd)]
    return list(zip([dot(t_even, x) for x in plus], [dot(t_odd, x) for x in minus]))


def inverse(items, tabs):
    a_even, t_even, a_odd, t_odd = tabs
    h = a_even.shape[0] // 2

    def side(x, k):
        lanes = slice(k * h, (k + 1) * h)
        return jnp.concatenate(
            [jnp.concatenate([part[:h, lanes], part[h:, lanes]], 1) for part in x], 0
        )

    even = [dot(side(x, 0), t_even) for x in items]
    odd = [dot(side(x, 1), t_odd) for x in items]
    plus = [a + b for a, b in zip(even, odd)]
    minus = [a - b for a, b in zip(even, odd)]
    low = [dot(a_even, quads(a[:h], b[:h], h).astype(bf16)) for a, b in zip(plus, minus)]
    high = [dot(a_odd, quads(a[h:], b[h:], h).astype(bf16)) for a, b in zip(plus, minus)]
    out = []
    for a, b in zip(low, high):
        s, d = a + b, a - b
        out.append(
            (jnp.concatenate([s[:h], d[:h]], 0), jnp.concatenate([s[h:], d[h:]], 0))
        )
    return out


def product(a, b):
    return a[0] * b[0] - a[1] * b[1], a[0] * b[1] + a[1] * b[0]


def product_conj(a, b):
    return a[0] * b[0] + a[1] * b[1], a[0] * b[1] - a[1] * b[0]


def halves(x, h=COLS):
    return (x[0][:, :h], x[1][:, :h]), (x[0][:, h:], x[1][:, h:])


def by_kernel(field, kernel_ref, conjugate):
    out = []
    h = field[0].shape[0] // 2
    op = product_conj if conjugate else product
    for k, part in enumerate(field):
        rows = slice(k * h, (k + 1) * h)
        spread = op((kernel_ref[0, rows, :], kernel_ref[1, rows, :]), (part[:h], part[h:]))
        out.append(jnp.concatenate(spread, 0).astype(bf16))
    return out


def window(rows_ref, top, col, extent):
    return tuple(
        tuple(rows_ref[plane, col + j, pl.ds(top, extent), :] for plane in (0, 1)) for j in (0, 1)
    )


def load_rows(here_ref, next_ref, rows_ref):
    count, _, _, height, _ = here_ref.shape
    for side, ref in enumerate((here_ref, next_ref)):
        for k in range(count):
            start = (side * count + k) * height
            rows_ref[:, :, start : start + height, :] = ref[k].astype(f32)


def add_window(totals_ref, top, col, term):
    extent = term[0][0].shape[0]
    for j in (0, 1):
        for plane in (0, 1):
            place = (plane, col + j, pl.ds(top, extent), slice(None))
            totals_ref[place] += term[j][plane]


def route_kernel(here_ref, owner_ref, row_ref, col_ref, images_ref, permute_ref, out_ref, meta_ref, second_ref):
    reads = images_ref.shape[0]
    tiles = out_ref.shape[1]
    tile_here, slab_here, slabs = here_ref[0], here_ref[1], here_ref[2]
    mine = (tile_here * slabs + slab_here) * reads

    def pack(i, _):
        owner = owner_ref[mine + i]
        rank = jnp.int32(0)
        rank = lax.fori_loop(
            0, i, lambda j, r: r + (owner_ref[mine + j] == owner).astype(jnp.int32), rank
        )
        image = images_ref[i]
        turned = dot(image, permute_ref[0]).astype(bf16)
        out_ref[rank, owner] = dot(permute_ref[1], turned).astype(bf16)
        return 0

    lax.fori_loop(0, reads, pack, 0)

    def clear(i, _):
        for f in range(4):
            meta_ref[f * K + i] = 0
        return 0

    lax.fori_loop(0, K, clear, 0)

    def sender(g, counts):
        base = (g * slabs + slab_here) * reads

        def read(i, state):
            first, later, seen = state
            match = (owner_ref[base + i] == tile_here).astype(jnp.int32)

            @pl.when((match == 1) & (seen == 0))
            def _():
                meta_ref[first] = g
                meta_ref[K + first] = row_ref[base + i]
                meta_ref[2 * K + first] = col_ref[base + i]

            @pl.when((match == 1) & (seen == 1))
            def _():
                second_ref[later] = tiles + g
                second_ref[K + later] = row_ref[base + i]
                second_ref[2 * K + later] = col_ref[base + i]

            fresh = match * (1 - seen)
            return first + fresh, later + match - fresh, seen + match

        first, later, _ = lax.fori_loop(0, reads, read, (counts[0], counts[1], jnp.int32(0)))
        return first, later

    first, later = lax.fori_loop(0, tiles, sender, (jnp.int32(0), jnp.int32(0)))

    def join(i, _):
        for f in range(3):
            meta_ref[f * K + first + i] = second_ref[f * K + i]
        return 0

    lax.fori_loop(0, later, join, 0)
    total = first + later
    meta_ref[4 * K] = total
    meta_ref[4 * K + 1] = first

    def target(i, _):
        meta_ref[3 * K + i] = jnp.where(i < total, meta_ref[K + i], 2 * images_ref.shape[1])
        return 0

    lax.fori_loop(0, K, target, 0)


def wave_kernel(meta_ref, here_ref, next_ref, probe_ref, kernel_ref, a0, t0, a1, t1, wave_ref, rows_ref):
    step = pl.program_id(0)
    extent = probe_ref.shape[0]

    @pl.when(step == 0)
    def _():
        load_rows(here_ref, next_ref, rows_ref)

    @pl.when(2 * step < meta_ref[4 * K])
    def _():
        tabs = a0[...], t0[...], a1[...], t1[...]
        probe = halves((probe_ref[:, :extent], probe_ref[:, extent:]))
        items = []
        for i in (0, 1):
            at = 2 * step + i
            w = window(rows_ref, meta_ref[K + at], meta_ref[2 * K + at], extent)
            items.append(tuple(product(p, q) for p, q in zip(probe, w)))
        spread = [by_kernel(x, kernel_ref, False) for x in forward(items, tabs)]
        for i, wave in enumerate(inverse(spread, tabs)):
            wave_ref[i, 0] = wave[0]
            wave_ref[i, 1] = wave[1]


def misfit_kernel(
    meta_ref, here_ref, next_ref, wave_ref, image0, image1, kernel_ref, a0, t0, a1, t1,
    back_ref, out_ref, rows_ref, totals_ref,
):
    step = pl.program_id(0)
    extent = image0.shape[1]
    h = extent // 2

    @pl.when(step == 0)
    def _():
        load_rows(here_ref, next_ref, rows_ref)
        totals_ref[...] = jnp.zeros_like(totals_ref)

    @pl.when(2 * step < meta_ref[4 * K])
    def _():
        tabs = a0[...], t0[...], a1[...], t1[...]
        items = []
        for i in (0, 1):
            at = 2 * step + i
            w = window(rows_ref, meta_ref[K + at], meta_ref[2 * K + at], extent)
            wave = halves((wave_ref[i, 0], wave_ref[i, 1]))
            items.append(tuple(product(p, q) for p, q in zip(wave, w)))
        far_grads = []
        for i, far in enumerate(forward(items, tabs)):
            image = (image0, image1)[i]
            parts = []
            for k, part in enumerate(far):
                re, im = part[:h], part[h:]
                misfit = re * re + im * im - image[0, k * h : (k + 1) * h, :].astype(f32)
                parts.append(jnp.concatenate([re * misfit, im * misfit], 0).astype(bf16))
            far_grads.append(parts)
        back = []
        for i, grad in enumerate(inverse(far_grads, tabs)):
            at = 2 * step + i
            grad = halves(grad)
            wave = halves((wave_ref[i, 0], wave_ref[i, 1]))
            col = meta_ref[2 * K + at]
            add_window(
                totals_ref, meta_ref[3 * K + at], col,
                [product_conj(p, q) for p, q in zip(wave, grad)],
            )
            w = window(rows_ref, meta_ref[K + at], col, extent)
            back.append(tuple(product_conj(p, q) for p, q in zip(w, grad)))
        for i, field in enumerate(forward(back, tabs)):
            for k, part in enumerate(by_kernel(field, kernel_ref, True)):
                back_ref[i, k] = part

    @pl.when(step == pl.num_programs(0) - 1)
    def _():
        out_ref[...] = totals_ref[:, :, : 2 * extent, :].astype(out_ref.dtype)


def exit_kernel(meta_ref, back_ref, probe_ref, a0, t0, a1, t1, out_ref, totals_ref):
    step = pl.program_id(0)
    extent = probe_ref.shape[0]

    @pl.when(step == 0)
    def _():
        totals_ref[...] = jnp.zeros_like(totals_ref)

    @pl.when(2 * step < meta_ref[4 * K])
    def _():
        tabs = a0[...], t0[...], a1[...], t1[...]
        probe = halves((probe_ref[:, :extent], probe_ref[:, extent:]))
        fields = [(back_ref[i, 0], back_ref[i, 1]) for i in (0, 1)]
        for i, grad in enumerate(inverse(fields, tabs)):
            at = 2 * step + i
            add_window(
                totals_ref, meta_ref[3 * K + at], meta_ref[2 * K + at],
                [product_conj(p, q) for p, q in zip(probe, halves(grad))],
            )

    @pl.when(step == pl.num_programs(0) - 1)
    def _():
        out_ref[...] = totals_ref[:, :, : 2 * extent, :].astype(out_ref.dtype)


def whole(shape):
    return pl.BlockSpec(shape, lambda *_: (0,) * len(shape))


VMEM = 56 * 1024 * 1024


def params():
    return pltpu.CompilerParams(vmem_limit_bytes=VMEM, dimension_semantics=("arbitrary",))


def route(images, here, owner_tile, row_offset, col_offset, permute, tiles):
    reads, extent = images.shape[:2]
    smem = pl.BlockSpec(memory_space=pltpu.SMEM)
    vmem = pl.BlockSpec(memory_space=pltpu.VMEM)
    return pl.pallas_call(
        route_kernel,
        in_specs=[smem, smem, smem, smem, vmem, vmem],
        out_specs=[vmem, smem],
        out_shape=[
            jax.ShapeDtypeStruct((CAP, tiles, extent, extent), bf16),
            jax.ShapeDtypeStruct((4 * K + 8,), jnp.int32),
        ],
        scratch_shapes=[pltpu.SMEM((4 * K,), jnp.int32)],
        compiler_params=pltpu.CompilerParams(vmem_limit_bytes=VMEM),
        name="route",
    )(here, owner_tile, row_offset, col_offset, images, permute)


def waves(meta, rows_here, rows_next, probe, kernel, tabs):
    extent = probe.shape[0]
    ins = [rows_here, rows_next, probe, kernel] + tabs
    total = 2 * extent
    return pl.pallas_call(
        wave_kernel,
        grid_spec=pltpu.PrefetchScalarGridSpec(
            num_scalar_prefetch=1,
            grid=(K // 2,),
            in_specs=[whole(x.shape) for x in ins],
            out_specs=pl.BlockSpec((2, 2, extent, extent), lambda i, m: (i, 0, 0, 0)),
            scratch_shapes=[pltpu.VMEM((2, rows_here.shape[2], total, COLS), f32)],
        ),
        out_shape=jax.ShapeDtypeStruct((K, 2, extent, extent), f32),
        compiler_params=params(),
        name="waves",
    )(meta, *ins)


def misfits(meta, rows_here, rows_next, wave, images, kernel, tabs):
    extent = images.shape[1]
    total = 2 * extent
    blocks = rows_here.shape[2]
    once = [rows_here, rows_next]
    tail = [kernel] + tabs
    pair = pl.BlockSpec((2, 2, extent, extent), lambda i, m: (i, 0, 0, 0))
    one = [
        pl.BlockSpec((1, extent, extent), lambda i, m, k=k: (m[2 * i + k], 0, 0)) for k in (0, 1)
    ]
    return pl.pallas_call(
        misfit_kernel,
        grid_spec=pltpu.PrefetchScalarGridSpec(
            num_scalar_prefetch=1,
            grid=(K // 2,),
            in_specs=[whole(x.shape) for x in once] + [pair] + one + [whole(x.shape) for x in tail],
            out_specs=[pair, whole((2, blocks, total, COLS))],
            scratch_shapes=[
                pltpu.VMEM((2, blocks, total, COLS), f32),
                pltpu.VMEM((2, blocks, total + extent, COLS), f32),
            ],
        ),
        out_shape=[
            jax.ShapeDtypeStruct((K, 2, extent, extent), bf16),
            jax.ShapeDtypeStruct((2, blocks, total, COLS), f32),
        ],
        compiler_params=params(),
        name="misfits",
    )(meta, *once, wave, images, images, *tail)


def exits(meta, back, probe, tabs, blocks):
    extent = probe.shape[0]
    total = 2 * extent
    pair = pl.BlockSpec((2, 2, extent, extent), lambda i, m: (i, 0, 0, 0))
    tail = [probe] + tabs
    return pl.pallas_call(
        exit_kernel,
        grid_spec=pltpu.PrefetchScalarGridSpec(
            num_scalar_prefetch=1,
            grid=(K // 2,),
            in_specs=[pair] + [whole(x.shape) for x in tail],
            out_specs=whole((2, blocks, total, COLS)),
            scratch_shapes=[pltpu.VMEM((2, blocks, total + extent, COLS), f32)],
        ),
        out_shape=jax.ShapeDtypeStruct((2, blocks, total, COLS), f32),
        compiler_params=params(),
        name="exits",
    )(meta, back, *tail)


def passed_along(value, axis, steps):
    count = lax.axis_size(axis)
    pairs = [(source, (source + steps) % count) for source in range(count)]
    return lax.ppermute(value, axis, pairs)


def shards(intensities, object_field, probe_wave, owner_tile, row_offset, col_offset):
    tile_count = lax.axis_size("tile")
    slab_count = lax.axis_size("slab")
    extent = intensities.shape[1]
    depth, _, height, width = object_field.shape
    blocks = width // COLS
    tabs, kernel, permute = make_tables(extent)
    here = jnp.stack(
        [lax.axis_index("tile"), lax.axis_index("slab"), jnp.int32(slab_count)]
    ).astype(jnp.int32)
    packed, meta = route(
        intensities, here, owner_tile, row_offset, col_offset,
        jnp.stack([permute, permute.T]), tile_count,
    )
    images = [
        lax.all_to_all(packed[rank], "tile", split_axis=0, concat_axis=0, tiled=True)
        for rank in range(CAP)
    ]
    images = jnp.concatenate(images, 0)
    own = jnp.transpose(
        object_field.reshape(depth, 2, height, blocks, COLS), (0, 1, 3, 2, 4)
    ).astype(bf16)
    gathered = [lax.all_gather(own[s], "slab", axis=0, tiled=False) for s in range(depth)]
    following = [passed_along(rows, "tile", -1) for rows in gathered]
    wave = waves(meta, gathered[0], following[0], probe_wave, kernel, tabs)
    back, total1 = misfits(meta, gathered[1], following[1], wave, images, kernel, tabs)
    total0 = exits(meta, back, probe_wave, tabs, blocks)
    grads = []
    tile_rows = height * slab_count
    for total in (total0, total1):
        moved = passed_along(total[:, :, tile_rows:].astype(bf16), "tile", 1)
        combined = total[:, :, :tile_rows] + moved.astype(f32)
        grads.append(lax.psum_scatter(combined, "slab", scatter_dimension=2, tiled=True))
    gradient = jnp.stack(grads)
    return jnp.transpose(gradient, (0, 1, 3, 2, 4)).reshape(depth, 2, height, width)


def solution(mesh):
    placed = (
        P(("tile", "slab"), None, None),
        P(None, None, ("tile", "slab"), None),
        P(),
        P(),
        P(),
        P(),
    )
    return jax.shard_map(
        shards,
        mesh=mesh,
        in_specs=placed,
        out_specs=P(None, None, ("tile", "slab"), None),
        check_vma=False,
    )
```

```python
import functools
import math

import jax
import jax.numpy as jnp
import ml_dtypes
import numpy as np
from jax import lax
from jax.experimental import pallas as pl
from jax.experimental.pallas import tpu as pltpu
from jax.sharding import PartitionSpec as P

K = 16
CAP = 2
COLS = 128
chirp_strength = 40.0
bf16 = jnp.bfloat16
f32 = jnp.float32


def make_tables(extent):
    counter = np.arange(extent, dtype=np.int64)
    angles = (counter[:, None] * counter[None, :] % extent).astype(np.float32) * np.float32(
        2.0 * math.pi / extent
    )
    scaling = np.float32(1.0 / math.sqrt(extent))
    cosine = (np.cos(angles) * scaling).astype(ml_dtypes.bfloat16)
    sine_part = (np.sin(angles) * scaling).astype(ml_dtypes.bfloat16)
    half = extent // 2
    tables = []
    for parity in (0, 1):
        c, s = cosine[:half, parity::2], sine_part[:half, parity::2]
        table = np.concatenate([np.concatenate([c, -s], 1), np.concatenate([s, c], 1)], 0)
        tables += [table, np.ascontiguousarray(table.T)]
    order = np.concatenate([counter[0::2], counter[1::2]])
    frequency = (((counter + half) % extent - half).astype(np.float32) / extent)[order]
    phases = np.float32(chirp_strength) * (frequency[:, None] ** 2 + frequency[None, :] ** 2)
    kernel = np.stack([np.cos(phases), -np.sin(phases)]).astype(np.float32)
    permute = (counter[:, None] == order[None, :]).astype(ml_dtypes.bfloat16)
    return [jnp.asarray(t) for t in tables], jnp.asarray(kernel), jnp.asarray(permute)


def dot(a, b):
    return jnp.dot(a, b, preferred_element_type=f32)


def quads(a, b, h):
    return jnp.concatenate(
        [
            jnp.concatenate([a[:, :h], b[:, :h]], 1),
            jnp.concatenate([a[:, h:], b[:, h:]], 1),
        ],
        0,
    )


def forward(items, tabs):
    a_even, t_even, a_odd, t_odd = tabs
    h = a_even.shape[0] // 2
    sums = [jnp.concatenate([l[0] + r[0], l[1] + r[1]], 1).astype(bf16) for l, r in items]
    diffs = [jnp.concatenate([l[0] - r[0], l[1] - r[1]], 1).astype(bf16) for l, r in items]
    even = [dot(x, a_even) for x in sums]
    odd = [dot(x, a_odd) for x in diffs]
    plus = [quads(a[:h] + a[h:], b[:h] + b[h:], h).astype(bf16) for a, b in zip(even, odd)]
    minus = [quads(a[:h] - a[h:], b[:h] - b[h:], h).astype(bf16) for a, b in zip(even, odd)]
    return list(zip([dot(t_even, x) for x in plus], [dot(t_odd, x) for x in minus]))


def inverse(items, tabs):
    a_even, t_even, a_odd, t_odd = tabs
    h = a_even.shape[0] // 2

    def side(x, k):
        lanes = slice(k * h, (k + 1) * h)
        return jnp.concatenate(
            [jnp.concatenate([part[:h, lanes], part[h:, lanes]], 1) for part in x], 0
        )

    even = [dot(side(x, 0), t_even) for x in items]
    odd = [dot(side(x, 1), t_odd) for x in items]
    plus = [a + b for a, b in zip(even, odd)]
    minus = [a - b for a, b in zip(even, odd)]
    low = [dot(a_even, quads(a[:h], b[:h], h).astype(bf16)) for a, b in zip(plus, minus)]
    high = [dot(a_odd, quads(a[h:], b[h:], h).astype(bf16)) for a, b in zip(plus, minus)]
    out = []
    for a, b in zip(low, high):
        s, d = a + b, a - b
        out.append(
            (jnp.concatenate([s[:h], d[:h]], 0), jnp.concatenate([s[h:], d[h:]], 0))
        )
    return out


def product(a, b):
    return a[0] * b[0] - a[1] * b[1], a[0] * b[1] + a[1] * b[0]


def product_conj(a, b):
    return a[0] * b[0] + a[1] * b[1], a[0] * b[1] - a[1] * b[0]


def halves(x, h=COLS):
    return (x[0][:, :h], x[1][:, :h]), (x[0][:, h:], x[1][:, h:])


def by_kernel(field, kernel_ref, conjugate):
    out = []
    h = field[0].shape[0] // 2
    op = product_conj if conjugate else product
    for k, part in enumerate(field):
        rows = slice(k * h, (k + 1) * h)
        spread = op((kernel_ref[0, rows, :], kernel_ref[1, rows, :]), (part[:h], part[h:]))
        out.append(jnp.concatenate(spread, 0).astype(bf16))
    return out


def window(rows_ref, top, col, extent):
    return tuple(
        tuple(rows_ref[plane, col + j, pl.ds(top, extent), :] for plane in (0, 1)) for j in (0, 1)
    )


def load_rows(slab_here, chunks, rows_ref):
    joined = len(chunks[0].shape) == 5
    count = len(chunks) if joined else len(chunks) // 2
    height = chunks[0].shape[-2]
    for side in (0, 1):
        for k in range(count):
            place = lax.rem(slab_here + count - k, count)
            start = pl.multiple_of((side * count + place) * height, height)
            shard = chunks[k][side] if joined else chunks[side * count + k][...]
            rows_ref[:, :, pl.ds(start, height), :] = shard.astype(f32)


def add_window(totals_ref, top, col, term):
    extent = term[0][0].shape[0]
    for j in (0, 1):
        for plane in (0, 1):
            place = (plane, col + j, pl.ds(top, extent), slice(None))
            totals_ref[place] += term[j][plane]


def route_kernel(here_ref, owner_ref, row_ref, col_ref, images_ref, permute_ref, out_ref, meta_ref, second_ref, turned_ref):
    reads, extent, _ = images_ref.shape
    tiles = out_ref.shape[0] // CAP
    tile_here, slab_here, slabs = here_ref[0], here_ref[1], here_ref[2]
    mine = (tile_here * slabs + slab_here) * reads

    owners = [owner_ref[mine + i] for i in range(reads)]
    for i in range(reads):
        turned_ref[i] = dot(images_ref[i], permute_ref[0]).astype(bf16)
    for i in range(reads):
        rank = jnp.int32(0)
        for j in range(i):
            rank += (owners[j] == owners[i]).astype(jnp.int32)
        out_ref[owners[i] * CAP + rank] = dot(permute_ref[1], turned_ref[i]).astype(bf16)

    def sender(g, counts):
        base = (g * slabs + slab_here) * reads
        first, later = counts
        seen = jnp.int32(0)
        for i in range(reads):
            match = (owner_ref[base + i] == tile_here).astype(jnp.int32)
            meta_ref[first] = base + i
            second_ref[later] = base + i
            fresh = match * (1 - seen)
            first, later, seen = first + fresh, later + match - fresh, seen + match
        return first, later

    first, later = lax.fori_loop(0, tiles, sender, (jnp.int32(0), jnp.int32(0)))
    total = first + later
    for i in range(K):
        in_first = i < first
        live = i < total
        row = jnp.where(in_first, meta_ref[i], second_ref[jnp.maximum(i - first, 0)])
        row = jnp.where(live, row, 0)
        group = row // (slabs * reads)
        meta_ref[i] = group * CAP + jnp.where(in_first, 0, 1)
        meta_ref[K + i] = row_ref[row]
        meta_ref[2 * K + i] = col_ref[row]
        meta_ref[3 * K + i] = jnp.where(live, row_ref[row], 2 * extent)
    meta_ref[4 * K] = total
    meta_ref[4 * K + 1] = first
    meta_ref[4 * K + 2] = slab_here


def give_totals(totals_ref, own_ref, lower_ref):
    rows = own_ref.shape[2]
    own_ref[...] = totals_ref[:, :, :rows, :]
    lower_ref[...] = totals_ref[:, :, rows : 2 * rows, :].astype(bf16)


def combine_kernel(here_ref, own_ref, moved_ref, mine_ref, *send_refs):
    height = mine_ref.shape[2]
    count = len(send_refs) + 1
    for k in range(count):
        place = lax.rem(here_ref[1] + k, count)
        rows = pl.ds(pl.multiple_of(place * height, height), height)
        both = own_ref[:, :, rows, :] + moved_ref[:, :, rows, :].astype(f32)
        if k == 0:
            mine_ref[...] = both
        else:
            send_refs[k - 1][...] = both.astype(bf16)


def finish_kernel(count, *refs):
    out_ref = refs[-1]
    for s in range(out_ref.shape[0]):
        parts = refs[s * count : (s + 1) * count]
        for plane in (0, 1):
            for block in range(parts[0].shape[1]):
                total = parts[0][plane, block]
                for part in parts[1:]:
                    total = total + part[plane, block].astype(f32)
                out_ref[s, plane, :, block * COLS : (block + 1) * COLS] = total


def pair_loop(meta_ref, body):
    def step(i, carry):
        body(2 * i, 2 * i + 1)
        return carry

    lax.fori_loop(0, lax.div(meta_ref[4 * K] + 1, 2), step, 0)


def wave_kernel(count, meta_ref, *refs):
    chunks, (probe_ref, kernel_ref, a0, t0, a1, t1, wave_ref, rows_ref) = refs[:count], refs[count:]
    extent = probe_ref.shape[0]
    load_rows(meta_ref[4 * K + 2], chunks, rows_ref)

    def body(*pair):
        tabs = a0[...], t0[...], a1[...], t1[...]
        probe = halves((probe_ref[:, :extent], probe_ref[:, extent:]))
        items = []
        for at in pair:
            w = window(rows_ref, meta_ref[K + at], meta_ref[2 * K + at], extent)
            items.append(tuple(product(p, q) for p, q in zip(probe, w)))
        spread = [by_kernel(x, kernel_ref, False) for x in forward(items, tabs)]
        for at, wave in zip(pair, inverse(spread, tabs)):
            wave_ref[at, 0] = wave[0]
            wave_ref[at, 1] = wave[1]

    pair_loop(meta_ref, body)


def misfit_kernel(count, meta_ref, *refs):
    chunks = refs[:count]
    wave_ref, images_ref, kernel_ref, a0, t0, a1, t1 = refs[count : count + 7]
    back_ref, own_ref, lower_ref, rows_ref, totals_ref = refs[count + 7 :]
    extent = images_ref.shape[1]
    h = extent // 2
    load_rows(meta_ref[4 * K + 2], chunks, rows_ref)
    totals_ref[...] = jnp.zeros_like(totals_ref)

    def body(*pair):
        tabs = a0[...], t0[...], a1[...], t1[...]
        items = []
        for at in pair:
            w = window(rows_ref, meta_ref[K + at], meta_ref[2 * K + at], extent)
            wave = halves((wave_ref[at, 0], wave_ref[at, 1]))
            items.append(tuple(product(p, q) for p, q in zip(wave, w)))
        far_grads = []
        for at, far in zip(pair, forward(items, tabs)):
            slot = meta_ref[at]
            parts = []
            for k, part in enumerate(far):
                re, im = part[:h], part[h:]
                image = images_ref[slot, k * h : (k + 1) * h, :].astype(f32)
                misfit = re * re + im * im - image
                parts.append(jnp.concatenate([re * misfit, im * misfit], 0).astype(bf16))
            far_grads.append(parts)
        back = []
        for at, grad in zip(pair, inverse(far_grads, tabs)):
            grad = halves(grad)
            wave = halves((wave_ref[at, 0], wave_ref[at, 1]))
            col = meta_ref[2 * K + at]
            add_window(
                totals_ref, meta_ref[3 * K + at], col,
                [product_conj(p, q) for p, q in zip(wave, grad)],
            )
            w = window(rows_ref, meta_ref[K + at], col, extent)
            back.append(tuple(product_conj(p, q) for p, q in zip(w, grad)))
        for at, field in zip(pair, forward(back, tabs)):
            for k, part in enumerate(by_kernel(field, kernel_ref, True)):
                back_ref[at, k] = part

    pair_loop(meta_ref, body)
    give_totals(totals_ref, own_ref, lower_ref)


def exit_kernel(meta_ref, back_ref, probe_ref, a0, t0, a1, t1, own_ref, lower_ref, totals_ref):
    extent = probe_ref.shape[0]
    totals_ref[...] = jnp.zeros_like(totals_ref)

    def body(*pair):
        tabs = a0[...], t0[...], a1[...], t1[...]
        probe = halves((probe_ref[:, :extent], probe_ref[:, extent:]))
        fields = [(back_ref[at, 0], back_ref[at, 1]) for at in pair]
        for at, grad in zip(pair, inverse(fields, tabs)):
            add_window(
                totals_ref, meta_ref[3 * K + at], meta_ref[2 * K + at],
                [product_conj(p, q) for p, q in zip(probe, halves(grad))],
            )

    pair_loop(meta_ref, body)
    give_totals(totals_ref, own_ref, lower_ref)


VMEM = 32 * 1024 * 1024


def call(kernel, name, ins, outs, scratch, estimate):
    smem = pl.BlockSpec(memory_space=pltpu.SMEM)
    vmem = pl.BlockSpec(memory_space=pltpu.VMEM)
    single = not isinstance(outs, list)
    return pl.pallas_call(
        kernel,
        in_specs=[smem if x.dtype == jnp.int32 else vmem for x in ins],
        out_specs=vmem if single else [smem if x.dtype == jnp.int32 else vmem for x in outs],
        out_shape=outs,
        scratch_shapes=scratch,
        compiler_params=pltpu.CompilerParams(vmem_limit_bytes=VMEM),
        cost_estimate=estimate,
        name=name,
    )(*ins)


def cost(transforms, extent):
    return pl.CostEstimate(
        flops=int(K * transforms * 8 * 2 * extent**3), bytes_accessed=0, transcendentals=0
    )


def route(images, here, owner_tile, row_offset, col_offset, permute, tiles):
    reads, extent = images.shape[:2]
    outs = [
        jax.ShapeDtypeStruct((CAP * tiles, extent, extent), bf16),
        jax.ShapeDtypeStruct((4 * K + 8,), jnp.int32),
    ]
    scratch = [pltpu.SMEM((K + 8,), jnp.int32), pltpu.VMEM(images.shape, bf16)]
    ins = [here, owner_tile, row_offset, col_offset, images, permute]
    return call(route_kernel, "route", ins, outs, scratch, cost(0.25, extent))


def waves(meta, chunks, probe, kernel, tabs):
    extent = probe.shape[0]
    return call(
        functools.partial(wave_kernel, len(chunks)),
        "waves",
        [meta] + chunks + [probe, kernel] + tabs,
        jax.ShapeDtypeStruct((K, 2, extent, extent), f32),
        [pltpu.VMEM((2, chunks[0].shape[-3], 2 * extent, COLS), f32)],
        cost(2, extent),
    )


def totals_out(extent, blocks):
    shape = (2, blocks, extent, COLS)
    outs = [jax.ShapeDtypeStruct(shape, f32), jax.ShapeDtypeStruct(shape, bf16)]
    return outs, pltpu.VMEM((2, blocks, 3 * extent, COLS), f32)


def misfits(meta, chunks, wave, images, kernel, tabs):
    extent = images.shape[1]
    blocks = chunks[0].shape[-3]
    outs, totals = totals_out(extent, blocks)
    return call(
        functools.partial(misfit_kernel, len(chunks)),
        "misfits",
        [meta] + chunks + [wave, images, kernel] + tabs,
        [jax.ShapeDtypeStruct((K, 2, extent, extent), bf16)] + outs,
        [pltpu.VMEM((2, blocks, 2 * extent, COLS), f32), totals],
        cost(3, extent),
    )


def exits(meta, back, probe, tabs, blocks):
    extent = probe.shape[0]
    outs, totals = totals_out(extent, blocks)
    return call(
        exit_kernel, "exits", [meta, back, probe] + tabs, outs, [totals], cost(1, extent)
    )


def combine(here, own, moved, count):
    shape = own.shape[:2] + (own.shape[2] // count, COLS)
    outs = [jax.ShapeDtypeStruct(shape, f32 if k == 0 else bf16) for k in range(count)]
    return call(combine_kernel, "combine", [here, own, moved], outs, [], None)


def finish(parts, count):
    blocks, height = parts[0].shape[1:3]
    out = jax.ShapeDtypeStruct((len(parts) // count, 2, height, blocks * COLS), f32)
    return call(functools.partial(finish_kernel, count), "finish", parts, out, [], None)


def passed_along(value, axis, steps):
    count = lax.axis_size(axis)
    pairs = [(source, (source + steps) % count) for source in range(count)]
    return lax.ppermute(value, axis, pairs)


def shards(intensities, object_field, probe_wave, owner_tile, row_offset, col_offset):
    tile_count = lax.axis_size("tile")
    slab_count = lax.axis_size("slab")
    extent = intensities.shape[1]
    depth, _, height, width = object_field.shape
    blocks = width // COLS
    tabs, kernel, permute = make_tables(extent)
    here = jnp.stack(
        [lax.axis_index("tile"), lax.axis_index("slab"), jnp.int32(slab_count)]
    ).astype(jnp.int32)
    own = jnp.transpose(
        object_field.reshape(depth, 2, height, blocks, COLS), (0, 1, 3, 2, 4)
    ).astype(bf16)
    following = passed_along(own, "tile", -1)
    packed, meta = route(
        intensities, here, owner_tile, row_offset, col_offset,
        jnp.stack([permute, permute.T]), tile_count,
    )
    packed, following = lax.optimization_barrier((packed, following))
    images = lax.all_to_all(packed, "tile", split_axis=0, concat_axis=0, tiled=True)
    first = [
        side[0] if k == 0 else passed_along(side[0], "slab", k)
        for side in (own, following)
        for k in range(slab_count)
    ]
    second = jnp.stack([own[1], following[1]])
    *first, second = lax.optimization_barrier((*first, second))
    second = [second if k == 0 else passed_along(second, "slab", k) for k in range(slab_count)]
    wave = waves(meta, first, probe_wave, kernel, tabs)
    back, own1, lower1 = misfits(meta, second, wave, images, kernel, tabs)
    own0, lower0 = exits(meta, back, probe_wave, tabs, blocks)
    parts = []
    for total, lower in ((own0, lower0), (own1, lower1)):
        moved = passed_along(lower, "tile", 1)
        mine, *sends = combine(here, total, moved, slab_count)
        parts.append(mine)
        parts += [passed_along(x, "slab", k + 1) for k, x in enumerate(sends)]
    return finish(parts, slab_count)


def solution(mesh):
    placed = (
        P(("tile", "slab"), None, None),
        P(None, None, ("tile", "slab"), None),
        P(),
        P(),
        P(),
        P(),
    )
    return jax.shard_map(
        shards,
        mesh=mesh,
        in_specs=placed,
        out_specs=P(None, None, ("tile", "slab"), None),
        check_vma=False,
    )
```

```python
import functools
import math

import jax
import jax.numpy as jnp
import ml_dtypes
import numpy as np
from jax import lax
from jax.experimental import pallas as pl
from jax.experimental.pallas import tpu as pltpu
from jax.sharding import PartitionSpec as P

K = 16
CAP = 2
GROUP = 4
COLS = 128
chirp_strength = 40.0
bf16 = jnp.bfloat16
f32 = jnp.float32


def make_tables(extent):
    counter = np.arange(extent, dtype=np.int64)
    angles = (counter[:, None] * counter[None, :] % extent).astype(np.float32) * np.float32(
        2.0 * math.pi / extent
    )
    scaling = np.float32(1.0 / math.sqrt(extent))
    cosine = (np.cos(angles) * scaling).astype(ml_dtypes.bfloat16)
    sine_part = (np.sin(angles) * scaling).astype(ml_dtypes.bfloat16)
    half = extent // 2
    tables = []
    for parity in (0, 1):
        c, s = cosine[:half, parity::2], sine_part[:half, parity::2]
        table = np.concatenate([np.concatenate([c, -s], 1), np.concatenate([s, c], 1)], 0)
        tables += [table, np.ascontiguousarray(table.T)]
    order = np.concatenate([counter[0::2], counter[1::2]])
    frequency = (((counter + half) % extent - half).astype(np.float32) / extent)[order]
    phases = np.float32(chirp_strength) * (frequency[:, None] ** 2 + frequency[None, :] ** 2)
    kernel = np.stack([np.cos(phases), -np.sin(phases)]).astype(np.float32)
    permute = (counter[:, None] == order[None, :]).astype(ml_dtypes.bfloat16)
    return [jnp.asarray(t) for t in tables], jnp.asarray(kernel), jnp.asarray(permute)


def dot(a, b):
    return jnp.dot(a, b, preferred_element_type=f32)


def row_dot(fields, table):
    n = fields[0].shape[0]
    out = dot(jnp.concatenate(fields, 0), table)
    return [out[i * n : (i + 1) * n] for i in range(len(fields))]


def quads(a, b, h):
    return jnp.concatenate(
        [
            jnp.concatenate([a[:, :h], b[:, :h]], 1),
            jnp.concatenate([a[:, h:], b[:, h:]], 1),
        ],
        0,
    )


def forward(items, tabs):
    a_even, t_even, a_odd, t_odd = tabs
    h = a_even.shape[0] // 2
    sums = [jnp.concatenate([l[0] + r[0], l[1] + r[1]], 1).astype(bf16) for l, r in items]
    diffs = [jnp.concatenate([l[0] - r[0], l[1] - r[1]], 1).astype(bf16) for l, r in items]
    even = row_dot(sums, a_even)
    odd = row_dot(diffs, a_odd)
    plus = [quads(a[:h] + a[h:], b[:h] + b[h:], h).astype(bf16) for a, b in zip(even, odd)]
    minus = [quads(a[:h] - a[h:], b[:h] - b[h:], h).astype(bf16) for a, b in zip(even, odd)]
    return list(zip([dot(t_even, x) for x in plus], [dot(t_odd, x) for x in minus]))


def inverse(items, tabs):
    a_even, t_even, a_odd, t_odd = tabs
    h = a_even.shape[0] // 2

    def side(x, k):
        lanes = slice(k * h, (k + 1) * h)
        return jnp.concatenate(
            [jnp.concatenate([part[:h, lanes], part[h:, lanes]], 1) for part in x], 0
        )

    even = row_dot([side(x, 0) for x in items], t_even)
    odd = row_dot([side(x, 1) for x in items], t_odd)
    plus = [a + b for a, b in zip(even, odd)]
    minus = [a - b for a, b in zip(even, odd)]
    low = [dot(a_even, quads(a[:h], b[:h], h).astype(bf16)) for a, b in zip(plus, minus)]
    high = [dot(a_odd, quads(a[h:], b[h:], h).astype(bf16)) for a, b in zip(plus, minus)]
    out = []
    for a, b in zip(low, high):
        s, d = a + b, a - b
        out.append(
            (jnp.concatenate([s[:h], d[:h]], 0), jnp.concatenate([s[h:], d[h:]], 0))
        )
    return out


def product(a, b):
    return a[0] * b[0] - a[1] * b[1], a[0] * b[1] + a[1] * b[0]


def product_conj(a, b):
    return a[0] * b[0] + a[1] * b[1], a[0] * b[1] - a[1] * b[0]


def halves(x, h=COLS):
    return (x[0][:, :h], x[1][:, :h]), (x[0][:, h:], x[1][:, h:])


def by_kernel(field, kernel_ref, conjugate):
    out = []
    h = field[0].shape[0] // 2
    op = product_conj if conjugate else product
    for k, part in enumerate(field):
        rows = slice(k * h, (k + 1) * h)
        spread = op((kernel_ref[0, rows, :], kernel_ref[1, rows, :]), (part[:h], part[h:]))
        out.append(jnp.concatenate(spread, 0).astype(bf16))
    return out


def window(rows_ref, top, col, extent):
    return tuple(
        tuple(rows_ref[plane, col + j, pl.ds(top, extent), :] for plane in (0, 1)) for j in (0, 1)
    )


def start_all(copies):
    for copy in copies:
        copy.start()
    return copies


def wait_all(copies):
    for copy in copies:
        copy.wait()


def copies_of(pairs, sems):
    return [pltpu.make_async_copy(a, b, sems.at[i]) for i, (a, b) in enumerate(pairs)]


def shard_copies(refs, shards):
    count = shards.shape[1]
    if len(refs) == count:
        return [(ref.at[side], shards.at[side, k]) for k, ref in enumerate(refs) for side in (0, 1)]
    return [(ref, shards.at[i // count, i % count]) for i, ref in enumerate(refs)]


def load_rows(slab_here, shards, rows_ref):
    count = shards.shape[1]
    height = shards.shape[-2]
    for side in (0, 1):
        for k in range(count):
            place = lax.rem(slab_here + count - k, count)
            start = pl.multiple_of((side * count + place) * height, height)
            rows_ref[:, :, pl.ds(start, height), :] = shards[side, k].astype(f32)


def group_count(meta_ref):
    return lax.div(meta_ref[4 * K] + GROUP - 1, GROUP)


def group_loop(meta_ref, ready, body, incoming=None, outgoing=None):
    last = group_count(meta_ref)

    def each(make, group, do):
        if make is not None:
            for copy in make(group, lax.rem(group, 2)):
                do(copy)

    @pl.when(last > 0)
    def _():
        each(incoming, 0, lambda c: c.start())

    ready()

    def step(group, carry):
        @pl.when(group + 1 < last)
        def _():
            each(incoming, group + 1, lambda c: c.start())

        each(incoming, group, lambda c: c.wait())

        @pl.when(group >= 2)
        def _():
            each(outgoing, group - 2, lambda c: c.wait())

        body([GROUP * group + j for j in range(GROUP)], group, lax.rem(group, 2))
        each(outgoing, group, lambda c: c.start())
        return carry

    lax.fori_loop(0, last, step, 0)
    for back in (2, 1):

        @pl.when(last >= back)
        def _():
            each(outgoing, last - back, lambda c: c.wait())


def add_window(totals_ref, top, col, term):
    extent = term[0][0].shape[0]
    for j in (0, 1):
        for plane in (0, 1):
            place = (plane, col + j, pl.ds(top, extent), slice(None))
            totals_ref[place] += term[j][plane]


def route_kernel(
    here_ref, owner_hbm, row_hbm, col_hbm, images_hbm, permute_hbm, out_hbm, meta_ref,
    owner_ref, row_ref, col_ref, second_ref, images_ref, permute_ref, turned_ref, packed_ref,
    sems, in_sems, out_sems,
):
    reads, extent, _ = images_ref.shape
    tiles = out_hbm.shape[0] // CAP
    tile_here, slab_here, slabs = here_ref[0], here_ref[1], here_ref[2]
    mine = (tile_here * slabs + slab_here) * reads
    small = copies_of(
        [(owner_hbm, owner_ref), (row_hbm, row_ref), (col_hbm, col_ref), (permute_hbm, permute_ref)], sems
    )
    start_all(small)
    arriving = copies_of([(images_hbm.at[i], images_ref.at[i]) for i in range(reads)], in_sems)
    start_all(arriving)
    wait_all(small)
    owners = [owner_ref[mine + i] for i in range(reads)]
    leaving = []
    for group in (range(reads // 2), range(reads // 2, reads)):
        for i in group:
            arriving[i].wait()
        for i in group:
            turned_ref[i] = dot(images_ref[i], permute_ref[0]).astype(bf16)
        for i in group:
            packed_ref[i] = dot(permute_ref[1], turned_ref[i]).astype(bf16)
        for i in group:
            rank = jnp.int32(0)
            for j in range(i):
                rank += (owners[j] == owners[i]).astype(jnp.int32)
            copy = pltpu.make_async_copy(
                packed_ref.at[i], out_hbm.at[owners[i] * CAP + rank], out_sems.at[i]
            )
            copy.start()
            leaving.append(copy)

    def sender(g, counts):
        base = (g * slabs + slab_here) * reads
        first, later = counts
        seen = jnp.int32(0)
        for i in range(reads):
            match = (owner_ref[base + i] == tile_here).astype(jnp.int32)
            meta_ref[first] = base + i
            second_ref[later] = base + i
            fresh = match * (1 - seen)
            first, later, seen = first + fresh, later + match - fresh, seen + match
        return first, later

    first, later = lax.fori_loop(0, tiles, sender, (jnp.int32(0), jnp.int32(0)))
    total = first + later
    for i in range(K):
        in_first = i < first
        live = i < total
        row = jnp.where(in_first, meta_ref[i], second_ref[jnp.maximum(i - first, 0)])
        row = jnp.where(live, row, 0)
        group = row // (slabs * reads)
        meta_ref[i] = group * CAP + jnp.where(in_first, 0, 1)
        meta_ref[K + i] = row_ref[row]
        meta_ref[2 * K + i] = col_ref[row]
        meta_ref[3 * K + i] = jnp.where(live, row_ref[row], 2 * extent)
    meta_ref[4 * K] = total
    meta_ref[4 * K + 1] = first
    meta_ref[4 * K + 2] = slab_here
    wait_all(leaving)


def give_lower(totals_ref, lower_ref):
    rows = lower_ref.shape[2]
    lower_ref[...] = totals_ref[:, :, rows : 2 * rows, :].astype(bf16)


def combine_kernel(here_ref, own_ref, moved_ref, mine_ref, *send_refs):
    height = mine_ref.shape[2]
    count = len(send_refs) + 1
    for k in range(count):
        place = lax.rem(here_ref[1] + k, count)
        rows = pl.ds(pl.multiple_of(place * height, height), height)
        both = own_ref[:, :, rows, :] + moved_ref[:, :, rows, :].astype(f32)
        if k == 0:
            mine_ref[...] = both
        else:
            send_refs[k - 1][...] = both.astype(bf16)


def finish_kernel(count, *refs):
    out_ref = refs[-1]
    for s in range(out_ref.shape[0]):
        parts = refs[s * count : (s + 1) * count]
        for plane in (0, 1):
            for block in range(parts[0].shape[1]):
                total = parts[0][plane, block]
                for part in parts[1:]:
                    total = total + part[plane, block].astype(f32)
                out_ref[s, plane, :, block * COLS : (block + 1) * COLS] = total


def tables_of(tabs_ref):
    return tuple(tabs_ref[i] for i in range(4))


def wave_kernel(count, meta_ref, *refs):
    rows_hbm = refs[:count]
    (probe_hbm, kernel_hbm, tabs_hbm, wave_ref,
     shards, probe_ref, kernel_ref, tabs, rows_ref, sems) = refs[count:]
    extent = probe_ref.shape[0]
    once = start_all(copies_of(
        shard_copies(rows_hbm, shards)
        + [(probe_hbm, probe_ref), (kernel_hbm, kernel_ref), (tabs_hbm, tabs)], sems))

    def ready():
        wait_all(once)
        load_rows(meta_ref[4 * K + 2], shards, rows_ref)

    def body(items, group, slot):
        tables = tables_of(tabs)
        probe = halves((probe_ref[:, :extent], probe_ref[:, extent:]))
        fields = []
        for at in items:
            w = window(rows_ref, meta_ref[K + at], meta_ref[2 * K + at], extent)
            fields.append(tuple(product(p, q) for p, q in zip(probe, w)))
        spread = [by_kernel(x, kernel_ref, False) for x in forward(fields, tables)]
        for at, wave in zip(items, inverse(spread, tables)):
            wave_ref[at, 0] = wave[0]
            wave_ref[at, 1] = wave[1]

    group_loop(meta_ref, ready, body)


def far_kernel(count, meta_ref, *refs):
    rows_hbm = refs[:count]
    (wave_ref, tabs_hbm, far_hbm, kept_hbm,
     shards, tabs, rows_ref, far_buf, kept_buf, sems, out_sems) = refs[count:]
    extent = wave_ref.shape[-1]
    once = start_all(copies_of(shard_copies(rows_hbm, shards) + [(tabs_hbm, tabs)], sems))

    def ready():
        wait_all(once)
        load_rows(meta_ref[4 * K + 2], shards, rows_ref)

    def outgoing(group, slot):
        return copies_of(
            [(far_buf.at[slot], far_hbm.at[group]), (kept_buf.at[slot], kept_hbm.at[group])], out_sems.at[slot]
        )

    def body(items, group, slot):
        fields = []
        for i, at in enumerate(items):
            w = window(rows_ref, meta_ref[K + at], meta_ref[2 * K + at], extent)
            wave = wave_ref[at, 0], wave_ref[at, 1]
            for plane in (0, 1):
                kept_buf[slot, i, plane] = wave[plane].astype(bf16)
            fields.append(tuple(product(p, q) for p, q in zip(halves(wave), w)))
        for i, far in enumerate(forward(fields, tables_of(tabs))):
            for k in (0, 1):
                far_buf[slot, i, k] = far[k]

    group_loop(meta_ref, ready, body, None, outgoing)


def misfit_kernel(count, meta_ref, *refs):
    rows_hbm = refs[:count]
    (kept_hbm, far_hbm, images_hbm, kernel_hbm, tabs_hbm, back_ref, totals_ref, lower_ref,
     shards, kernel_ref, tabs, rows_ref, kept_buf, far_buf, image_buf, sems, in_sems) = refs[count:]
    extent = images_hbm.shape[1]
    h = extent // 2
    once = start_all(copies_of(
        shard_copies(rows_hbm, shards) + [(kernel_hbm, kernel_ref), (tabs_hbm, tabs)], sems))

    def ready():
        totals_ref[...] = jnp.zeros_like(totals_ref)
        wait_all(once)
        load_rows(meta_ref[4 * K + 2], shards, rows_ref)

    def incoming(group, slot):
        return copies_of(
            [(kept_hbm.at[group], kept_buf.at[slot]), (far_hbm.at[group], far_buf.at[slot])]
            + [(images_hbm.at[meta_ref[GROUP * group + i]], image_buf.at[slot, i]) for i in range(GROUP)],
            in_sems.at[slot],
        )

    def body(items, group, slot):
        tables = tables_of(tabs)
        far_grads = []
        for i, at in enumerate(items):
            parts = []
            for k in (0, 1):
                re, im = far_buf[slot, i, k, :h], far_buf[slot, i, k, h:]
                image = image_buf[slot, i, k * h : (k + 1) * h, :].astype(f32)
                misfit = re * re + im * im - image
                parts.append(jnp.concatenate([re * misfit, im * misfit], 0).astype(bf16))
            far_grads.append(parts)
        back = []
        for i, (at, grad) in enumerate(zip(items, inverse(far_grads, tables))):
            grad = halves(grad)
            wave = halves((kept_buf[slot, i, 0].astype(f32), kept_buf[slot, i, 1].astype(f32)))
            col = meta_ref[2 * K + at]
            add_window(
                totals_ref, meta_ref[3 * K + at], col,
                [product_conj(p, q) for p, q in zip(wave, grad)],
            )
            w = window(rows_ref, meta_ref[K + at], col, extent)
            back.append(tuple(product_conj(p, q) for p, q in zip(w, grad)))
        for at, field in zip(items, forward(back, tables)):
            for k, part in enumerate(by_kernel(field, kernel_ref, True)):
                back_ref[at, k] = part

    group_loop(meta_ref, ready, body, incoming)
    give_lower(totals_ref, lower_ref)


def exit_kernel(meta_ref, back_ref, probe_hbm, tabs_hbm, totals_ref, lower_ref, probe_ref, tabs, sems):
    extent = probe_ref.shape[0]
    once = start_all(copies_of([(probe_hbm, probe_ref), (tabs_hbm, tabs)], sems))

    def ready():
        totals_ref[...] = jnp.zeros_like(totals_ref)
        wait_all(once)

    def body(items, group, slot):
        probe = halves((probe_ref[:, :extent], probe_ref[:, extent:]))
        fields = [(back_ref[at, 0], back_ref[at, 1]) for at in items]
        for at, grad in zip(items, inverse(fields, tables_of(tabs))):
            add_window(
                totals_ref, meta_ref[3 * K + at], meta_ref[2 * K + at],
                [product_conj(p, q) for p, q in zip(probe, halves(grad))],
            )

    group_loop(meta_ref, ready, body)
    give_lower(totals_ref, lower_ref)


MIB = 1024 * 1024
VMEM = 60 * MIB
LIMIT = 46 * MIB


smem = pl.BlockSpec(memory_space=pltpu.SMEM)
vmem = pl.BlockSpec(memory_space=pltpu.VMEM)
hbm = pl.BlockSpec(memory_space=pltpu.HBM)
anywhere = pl.BlockSpec(memory_space=pl.ANY)


def call(kernel, name, ins, in_specs, outs, out_specs, scratch, estimate=None, limit=VMEM):
    return pl.pallas_call(
        kernel,
        in_specs=in_specs,
        out_specs=out_specs,
        out_shape=outs,
        scratch_shapes=scratch,
        compiler_params=pltpu.CompilerParams(vmem_limit_bytes=limit),
        cost_estimate=estimate,
        name=name,
    )(*ins)


def cost(transforms, extent):
    return pl.CostEstimate(
        flops=int(K * transforms * 8 * 2 * extent**3), bytes_accessed=0, transcendentals=0
    )


def sems(*shape):
    return pltpu.SemaphoreType.DMA(shape)


def like(x):
    return pltpu.VMEM(x.shape, x.dtype)


def route(images, here, owner_tile, row_offset, col_offset, permute, tiles):
    reads, extent = images.shape[:2]
    outs = [
        pltpu.HBM((CAP * tiles, extent, extent), bf16),
        jax.ShapeDtypeStruct((4 * K + 8,), jnp.int32),
    ]
    numbers = pltpu.SMEM(owner_tile.shape, jnp.int32)
    scratch = [
        numbers, numbers, numbers, pltpu.SMEM((K + 8,), jnp.int32),
        like(images), like(permute), like(images), like(images), sems(4), sems(reads), sems(reads),
    ]
    ins = [here, owner_tile, row_offset, col_offset, images, permute]
    return call(route_kernel, "route", ins, [smem] + [hbm] * 5, outs, [hbm, smem], scratch, cost(0.25, extent))


def shards_scratch(rows, slabs):
    return pltpu.VMEM((2, slabs) + rows[0].shape[-4:], bf16)


def rows_padded(rows, slabs):
    planes, blocks, height, _ = rows[0].shape[-4:]
    return pltpu.VMEM((planes, blocks, 2 * slabs * height, COLS), f32)


def groups(extent, dtype):
    return pltpu.HBM((K // GROUP, GROUP, 2, extent, extent), dtype)


def group_buffer(extent, dtype):
    return pltpu.VMEM((2, GROUP, 2, extent, extent), dtype)


def waves(meta, rows, probe, kernel, tabs, slabs):
    extent = probe.shape[0]
    scratch = [
        shards_scratch(rows, slabs), like(probe), like(kernel), like(tabs), rows_padded(rows, slabs),
        sems(2 * slabs + 3),
    ]
    return call(
        functools.partial(wave_kernel, len(rows)), "waves", [meta] + rows + [probe, kernel, tabs],
        [smem] + [anywhere] * len(rows) + [hbm] * 3, pltpu.VMEM((K, 2, extent, extent), f32), vmem, scratch,
        cost(2, extent), limit=32 * MIB,
    )


def fars(meta, rows, wave, tabs, slabs):
    extent = wave.shape[-1]
    scratch = [
        shards_scratch(rows, slabs), like(tabs), rows_padded(rows, slabs),
        group_buffer(extent, f32), group_buffer(extent, bf16), sems(2 * slabs + 1), sems(2, 2),
    ]
    return call(
        functools.partial(far_kernel, len(rows)), "fars", [meta] + rows + [wave, tabs],
        [smem] + [anywhere] * len(rows) + [vmem, hbm], [groups(extent, f32), groups(extent, bf16)], [hbm, hbm],
        scratch, cost(1, extent), limit=32 * MIB,
    )


def totals_out(extent, blocks):
    return [
        pltpu.VMEM((2, blocks, 3 * extent, COLS), f32),
        jax.ShapeDtypeStruct((2, blocks, extent, COLS), bf16),
    ]


def misfits(meta, rows, kept, far, images, kernel, tabs, slabs):
    extent = images.shape[1]
    scratch = [
        shards_scratch(rows, slabs), like(kernel), like(tabs), rows_padded(rows, slabs),
        group_buffer(extent, bf16), group_buffer(extent, f32), pltpu.VMEM((2, GROUP, extent, extent), bf16),
        sems(2 * slabs + 2), sems(2, 2 + GROUP),
    ]
    return call(
        functools.partial(misfit_kernel, len(rows)), "misfits", [meta] + rows + [kept, far, images, kernel, tabs],
        [smem] + [anywhere] * len(rows) + [hbm, hbm, anywhere, hbm, hbm],
        [pltpu.VMEM((K, 2, extent, extent), bf16)] + totals_out(extent, rows[0].shape[-3]), [vmem, vmem, vmem],
        scratch, cost(2, extent), limit=LIMIT,
    )


def exits(meta, back, probe, tabs, blocks):
    extent = probe.shape[0]
    return call(
        exit_kernel, "exits", [meta, back, probe, tabs], [smem, vmem, hbm, hbm], totals_out(extent, blocks),
        [vmem, vmem], [like(probe), like(tabs), sems(2)], cost(1, extent), limit=LIMIT,
    )


def combine(here, own, moved, count):
    shape = own.shape[:2] + (moved.shape[2] // count, COLS)
    outs = [jax.ShapeDtypeStruct(shape, f32 if k == 0 else bf16) for k in range(count)]
    return call(combine_kernel, "combine", [here, own, moved], [smem, vmem, vmem], outs, [vmem] * count, [], limit=VMEM // 4)


def finish(parts, count):
    blocks, height = parts[0].shape[1:3]
    out = jax.ShapeDtypeStruct((len(parts) // count, 2, height, blocks * COLS), f32)
    return call(
        functools.partial(finish_kernel, count), "finish", parts, [vmem] * len(parts), out, vmem, [], limit=VMEM // 4
    )


def passed_along(value, axis, steps):
    count = lax.axis_size(axis)
    pairs = [(source, (source + steps) % count) for source in range(count)]
    return lax.ppermute(value, axis, pairs)


def shards(intensities, object_field, probe_wave, owner_tile, row_offset, col_offset):
    tile_count = lax.axis_size("tile")
    slab_count = lax.axis_size("slab")
    extent = intensities.shape[1]
    depth, _, height, width = object_field.shape
    blocks = width // COLS
    tabs, kernel, permute = make_tables(extent)
    here = jnp.stack(
        [lax.axis_index("tile"), lax.axis_index("slab"), jnp.int32(slab_count)]
    ).astype(jnp.int32)
    own = jnp.transpose(
        object_field.reshape(depth, 2, height, blocks, COLS), (0, 1, 3, 2, 4)
    ).astype(bf16)
    tabs = jnp.stack(tabs)
    following = passed_along(own, "tile", -1)
    packed, meta = route(
        intensities, here, owner_tile, row_offset, col_offset,
        jnp.stack([permute, permute.T]), tile_count,
    )
    def gather(rows):
        return [rows] + [passed_along(rows, "slab", k) for k in range(1, slab_count)]

    mine0 = gather(own[0])
    packed, following, *mine0 = lax.optimization_barrier((packed, following, *mine0))
    images = lax.all_to_all(packed, "tile", split_axis=0, concat_axis=0, tiled=True)
    next0 = gather(following[0])
    both = jnp.stack([own[1], following[1]])
    *next0, both = lax.optimization_barrier((*next0, both))
    first = mine0 + next0
    second = gather(both)
    wave = waves(meta, first, probe_wave, kernel, tabs, slab_count)
    far, kept = fars(meta, second, wave, tabs, slab_count)
    back, total1, lower1 = misfits(meta, second, kept, far, images, kernel, tabs, slab_count)
    total0, lower0 = exits(meta, back, probe_wave, tabs, blocks)
    parts = []
    for total, lower in ((total0, lower0), (total1, lower1)):
        moved = passed_along(lower, "tile", 1)
        mine, *sends = combine(here, total, moved, slab_count)
        parts.append(mine)
        parts += [passed_along(x, "slab", k + 1) for k, x in enumerate(sends)]
    return finish(parts, slab_count)


def solution(mesh):
    placed = (
        P(("tile", "slab"), None, None),
        P(None, None, ("tile", "slab"), None),
        P(),
        P(),
        P(),
        P(),
    )
    return jax.shard_map(
        shards,
        mesh=mesh,
        in_specs=placed,
        out_specs=P(None, None, ("tile", "slab"), None),
        check_vma=False,
    )
```

```python
import functools
import math

import jax
import jax.numpy as jnp
import ml_dtypes
import numpy as np
from jax import lax
from jax.experimental import pallas as pl
from jax.experimental.pallas import tpu as pltpu
from jax.sharding import PartitionSpec as P

K = 16
CAP = 2
GROUP = 4
COLS = 128
chirp_strength = 40.0
bf16 = jnp.bfloat16
f32 = jnp.float32


def make_tables(extent):
    counter = np.arange(extent, dtype=np.int64)
    angles = (counter[:, None] * counter[None, :] % extent).astype(np.float32) * np.float32(
        2.0 * math.pi / extent
    )
    scaling = np.float32(1.0 / math.sqrt(extent))
    cosine = (np.cos(angles) * scaling).astype(ml_dtypes.bfloat16)
    sine_part = (np.sin(angles) * scaling).astype(ml_dtypes.bfloat16)
    half = extent // 2
    tables = []
    for parity in (0, 1):
        c, s = cosine[:half, parity::2], sine_part[:half, parity::2]
        table = np.concatenate([np.concatenate([c, -s], 1), np.concatenate([s, c], 1)], 0)
        tables += [table, np.ascontiguousarray(table.T)]
    order = np.concatenate([counter[0::2], counter[1::2]])
    frequency = (((counter + half) % extent - half).astype(np.float32) / extent)[order]
    phases = np.float32(chirp_strength) * (frequency[:, None] ** 2 + frequency[None, :] ** 2)
    kernel = np.stack([np.cos(phases), -np.sin(phases)]).astype(np.float32)
    permute = (counter[:, None] == order[None, :]).astype(ml_dtypes.bfloat16)
    return [jnp.asarray(t) for t in tables], jnp.asarray(kernel), jnp.asarray(permute)


def dot(a, b):
    return jnp.dot(a, b, preferred_element_type=f32)


def row_dot(fields, table):
    n = fields[0].shape[0]
    out = dot(jnp.concatenate(fields, 0), table)
    return [out[i * n : (i + 1) * n] for i in range(len(fields))]


def quads(a, b, h):
    return jnp.concatenate(
        [
            jnp.concatenate([a[:, :h], b[:, :h]], 1),
            jnp.concatenate([a[:, h:], b[:, h:]], 1),
        ],
        0,
    )


def folded(field):
    l, r = field
    return (
        jnp.concatenate([l[0] + r[0], l[1] + r[1]], 1).astype(bf16),
        jnp.concatenate([l[0] - r[0], l[1] - r[1]], 1).astype(bf16),
    )


def forward(items, tabs):
    a_even, t_even, a_odd, t_odd = tabs
    h = a_even.shape[0] // 2
    even = row_dot([x[0] for x in items], a_even)
    odd = row_dot([x[1] for x in items], a_odd)
    plus = [quads(a[:h] + a[h:], b[:h] + b[h:], h).astype(bf16) for a, b in zip(even, odd)]
    minus = [quads(a[:h] - a[h:], b[:h] - b[h:], h).astype(bf16) for a, b in zip(even, odd)]
    return list(zip([dot(t_even, x) for x in plus], [dot(t_odd, x) for x in minus]))


def inverse(items, tabs):
    a_even, t_even, a_odd, t_odd = tabs
    h = a_even.shape[0] // 2

    def side(x, k):
        lanes = slice(k * h, (k + 1) * h)
        return jnp.concatenate(
            [jnp.concatenate([part[:h, lanes], part[h:, lanes]], 1) for part in x], 0
        )

    even = row_dot([side(x, 0) for x in items], t_even)
    odd = row_dot([side(x, 1) for x in items], t_odd)
    plus = [a + b for a, b in zip(even, odd)]
    minus = [a - b for a, b in zip(even, odd)]
    low = [dot(a_even, quads(a[:h], b[:h], h).astype(bf16)) for a, b in zip(plus, minus)]
    high = [dot(a_odd, quads(a[h:], b[h:], h).astype(bf16)) for a, b in zip(plus, minus)]
    out = []
    for a, b in zip(low, high):
        s, d = a + b, a - b
        out.append(
            (jnp.concatenate([s[:h], d[:h]], 0), jnp.concatenate([s[h:], d[h:]], 0))
        )
    return out


def product(a, b):
    return a[0] * b[0] - a[1] * b[1], a[0] * b[1] + a[1] * b[0]


def product_conj(a, b):
    return a[0] * b[0] + a[1] * b[1], a[0] * b[1] - a[1] * b[0]


def halves(x, h=COLS):
    return (x[0][:, :h], x[1][:, :h]), (x[0][:, h:], x[1][:, h:])


def by_kernel(field, kernel_ref, conjugate):
    out = []
    h = field[0].shape[0] // 2
    op = product_conj if conjugate else product
    for k, part in enumerate(field):
        rows = slice(k * h, (k + 1) * h)
        spread = op((kernel_ref[0, rows, :], kernel_ref[1, rows, :]), (part[:h], part[h:]))
        out.append(jnp.concatenate(spread, 0).astype(bf16))
    return out


def window(rows_ref, top, col, extent):
    return tuple(
        tuple(rows_ref[plane, col + j, pl.ds(top, extent), :] for plane in (0, 1)) for j in (0, 1)
    )


def start_all(copies):
    for copy in copies:
        copy.start()
    return copies


def wait_all(copies):
    for copy in copies:
        copy.wait()


def copies_of(pairs, sems):
    return [pltpu.make_async_copy(a, b, sems.at[i]) for i, (a, b) in enumerate(pairs)]


def shard_copies(refs, shards):
    count = shards.shape[1]
    if len(refs) == count:
        return [(ref.at[side], shards.at[side, k]) for k, ref in enumerate(refs) for side in (0, 1)]
    return [(ref, shards.at[i // count, i % count]) for i, ref in enumerate(refs)]


def load_rows(slab_here, shards, rows_ref):
    count = shards.shape[1]
    height = shards.shape[-2]
    for side in (0, 1):
        for k in range(count):
            place = lax.rem(slab_here + count - k, count)
            start = pl.multiple_of((side * count + place) * height, height)
            rows_ref[:, :, pl.ds(start, height), :] = shards[side, k].astype(f32)


def group_count(meta_ref):
    return lax.div(meta_ref[4 * K] + GROUP - 1, GROUP)


def group_loop(meta_ref, ready, body, incoming=None, outgoing=None):
    last = group_count(meta_ref)

    def each(make, group, do):
        if make is not None:
            for copy in make(group, lax.rem(group, 2)):
                do(copy)

    @pl.when(last > 0)
    def _():
        each(incoming, 0, lambda c: c.start())

    ready()

    def step(group, carry):
        @pl.when(group + 1 < last)
        def _():
            each(incoming, group + 1, lambda c: c.start())

        each(incoming, group, lambda c: c.wait())

        @pl.when(group >= 2)
        def _():
            each(outgoing, group - 2, lambda c: c.wait())

        body([GROUP * group + j for j in range(GROUP)], group, lax.rem(group, 2))
        each(outgoing, group, lambda c: c.start())
        return carry

    lax.fori_loop(0, last, step, 0)
    for back in (2, 1):

        @pl.when(last >= back)
        def _():
            each(outgoing, last - back, lambda c: c.wait())


def add_window(totals_ref, top, col, term):
    extent = term[0][0].shape[0]
    for j in (0, 1):
        for plane in (0, 1):
            place = (plane, col + j, pl.ds(top, extent), slice(None))
            totals_ref[place] += term[j][plane]


def route_kernel(
    here_ref, owner_hbm, row_hbm, col_hbm, images_hbm, permute_hbm, out_hbm, meta_ref,
    owner_ref, row_ref, col_ref, second_ref, images_ref, permute_ref, turned_ref, packed_ref,
    sems, in_sems, out_sems,
):
    reads, extent, _ = images_ref.shape
    tiles = out_hbm.shape[0] // CAP
    tile_here, slab_here, slabs = here_ref[0], here_ref[1], here_ref[2]
    mine = (tile_here * slabs + slab_here) * reads
    small = copies_of(
        [(owner_hbm, owner_ref), (row_hbm, row_ref), (col_hbm, col_ref), (permute_hbm, permute_ref)], sems
    )
    start_all(small)
    arriving = copies_of([(images_hbm.at[i], images_ref.at[i]) for i in range(reads)], in_sems)
    start_all(arriving)
    wait_all(small)
    owners = [owner_ref[mine + i] for i in range(reads)]
    leaving = []
    for group in (range(reads // 2), range(reads // 2, reads)):
        for i in group:
            arriving[i].wait()
        for i in group:
            turned_ref[i] = dot(images_ref[i], permute_ref[0]).astype(bf16)
        for i in group:
            packed_ref[i] = dot(permute_ref[1], turned_ref[i]).astype(bf16)
        for i in group:
            rank = jnp.int32(0)
            for j in range(i):
                rank += (owners[j] == owners[i]).astype(jnp.int32)
            copy = pltpu.make_async_copy(
                packed_ref.at[i], out_hbm.at[owners[i] * CAP + rank], out_sems.at[i]
            )
            copy.start()
            leaving.append(copy)

    def sender(g, counts):
        base = (g * slabs + slab_here) * reads
        first, later = counts
        seen = jnp.int32(0)
        for i in range(reads):
            match = (owner_ref[base + i] == tile_here).astype(jnp.int32)
            meta_ref[first] = base + i
            second_ref[later] = base + i
            fresh = match * (1 - seen)
            first, later, seen = first + fresh, later + match - fresh, seen + match
        return first, later

    first, later = lax.fori_loop(0, tiles, sender, (jnp.int32(0), jnp.int32(0)))
    total = first + later
    for i in range(K):
        in_first = i < first
        live = i < total
        row = jnp.where(in_first, meta_ref[i], second_ref[jnp.maximum(i - first, 0)])
        row = jnp.where(live, row, 0)
        group = row // (slabs * reads)
        meta_ref[i] = group * CAP + jnp.where(in_first, 0, 1)
        meta_ref[K + i] = row_ref[row]
        meta_ref[2 * K + i] = col_ref[row]
        meta_ref[3 * K + i] = jnp.where(live, row_ref[row], 2 * extent)
    meta_ref[4 * K] = total
    meta_ref[4 * K + 1] = first
    meta_ref[4 * K + 2] = slab_here
    wait_all(leaving)


def give_lower(totals_ref, lower_ref):
    rows = lower_ref.shape[2]
    lower_ref[...] = totals_ref[:, :, rows : 2 * rows, :].astype(bf16)


def combine_kernel(here_ref, own_ref, moved_ref, mine_ref, *send_refs):
    height = mine_ref.shape[2]
    count = len(send_refs) + 1
    for k in range(count):
        place = lax.rem(here_ref[1] + k, count)
        rows = pl.ds(pl.multiple_of(place * height, height), height)
        both = own_ref[:, :, rows, :] + moved_ref[:, :, rows, :].astype(f32)
        if k == 0:
            mine_ref[...] = both
        else:
            send_refs[k - 1][...] = both.astype(bf16)


def finish_kernel(count, *refs):
    out_ref = refs[-1]
    for s in range(out_ref.shape[0]):
        parts = refs[s * count : (s + 1) * count]
        for plane in (0, 1):
            for block in range(parts[0].shape[1]):
                total = parts[0][plane, block]
                for part in parts[1:]:
                    total = total + part[plane, block].astype(f32)
                out_ref[s, plane, :, block * COLS : (block + 1) * COLS] = total


def tables_of(tabs_ref):
    return tuple(tabs_ref[i] for i in range(4))


def wave_kernel(count, meta_ref, *refs):
    rows_hbm = refs[:count]
    (probe_hbm, kernel_hbm, tabs_hbm, wave_hbm,
     shards, probe_ref, kernel_ref, tabs, rows_ref, wave_buf, sems, out_sems) = refs[count:]
    extent = probe_ref.shape[0]
    once = start_all(copies_of(
        shard_copies(rows_hbm, shards)
        + [(probe_hbm, probe_ref), (kernel_hbm, kernel_ref), (tabs_hbm, tabs)], sems))

    def ready():
        wait_all(once)
        load_rows(meta_ref[4 * K + 2], shards, rows_ref)

    def outgoing(group, slot):
        return copies_of([(wave_buf.at[slot], wave_hbm.at[group])], out_sems.at[slot])

    def body(items, group, slot):
        tables = tables_of(tabs)
        probe = halves((probe_ref[:, :extent], probe_ref[:, extent:]))
        fields = []
        for at in items:
            w = window(rows_ref, meta_ref[K + at], meta_ref[2 * K + at], extent)
            fields.append(folded(tuple(product(p, q) for p, q in zip(probe, w))))
        spread = [by_kernel(x, kernel_ref, False) for x in forward(fields, tables)]
        for i, wave in enumerate(inverse(spread, tables)):
            wave_buf[slot, i, 0] = wave[0]
            wave_buf[slot, i, 1] = wave[1]

    group_loop(meta_ref, ready, body, None, outgoing)


def misfit_kernel(count, meta_ref, *refs):
    rows_hbm = refs[:count]
    (wave_hbm, images_hbm, tabs_hbm, back_ref, totals_ref, lower_ref,
     shards, tabs, rows_ref, wave_buf, image_buf, sems, in_sems) = refs[count:]
    extent = images_hbm.shape[1]
    h = extent // 2
    once = start_all(copies_of(shard_copies(rows_hbm, shards) + [(tabs_hbm, tabs)], sems))

    def ready():
        totals_ref[...] = jnp.zeros_like(totals_ref)
        wait_all(once)
        load_rows(meta_ref[4 * K + 2], shards, rows_ref)

    def incoming(group, slot):
        return copies_of(
            [(wave_hbm.at[group], wave_buf.at[slot])]
            + [(images_hbm.at[meta_ref[GROUP * group + i]], image_buf.at[slot, i]) for i in range(GROUP)],
            in_sems.at[slot],
        )

    def body(items, group, slot):
        tables = tables_of(tabs)

        def wave_of(i):
            return halves((wave_buf[slot, i, 0], wave_buf[slot, i, 1]))

        fields = []
        for i, at in enumerate(items):
            w = window(rows_ref, meta_ref[K + at], meta_ref[2 * K + at], extent)
            fields.append(folded(tuple(product(p, q) for p, q in zip(wave_of(i), w))))
        far_grads = []
        for i, far in enumerate(forward(fields, tables)):
            parts = []
            for k, part in enumerate(far):
                re, im = part[:h], part[h:]
                image = image_buf[slot, i, k * h : (k + 1) * h, :].astype(f32)
                misfit = re * re + im * im - image
                parts.append(jnp.concatenate([re * misfit, im * misfit], 0).astype(bf16))
            far_grads.append(parts)
        for i, (at, grad) in enumerate(zip(items, inverse(far_grads, tables))):
            grad = halves(grad)
            col = meta_ref[2 * K + at]
            add_window(
                totals_ref, meta_ref[3 * K + at], col,
                [product_conj(p, q) for p, q in zip(wave_of(i), grad)],
            )
            w = window(rows_ref, meta_ref[K + at], col, extent)
            back = folded(tuple(product_conj(p, q) for p, q in zip(w, grad)))
            for k in (0, 1):
                back_ref[at, k] = back[k]

    group_loop(meta_ref, ready, body, incoming)
    give_lower(totals_ref, lower_ref)


def back_kernel(meta_ref, fields_ref, kernel_hbm, tabs_hbm, back_ref, kernel_ref, tabs, sems):
    once = start_all(copies_of([(kernel_hbm, kernel_ref), (tabs_hbm, tabs)], sems))

    def ready():
        wait_all(once)

    def body(items, group, slot):
        fields = [(fields_ref[at, 0], fields_ref[at, 1]) for at in items]
        for at, field in zip(items, forward(fields, tables_of(tabs))):
            for k, part in enumerate(by_kernel(field, kernel_ref, True)):
                back_ref[at, k] = part

    group_loop(meta_ref, ready, body)


def exit_kernel(meta_ref, back_ref, probe_hbm, tabs_hbm, totals_ref, lower_ref, probe_ref, tabs, sems):
    extent = probe_ref.shape[0]
    once = start_all(copies_of([(probe_hbm, probe_ref), (tabs_hbm, tabs)], sems))

    def ready():
        totals_ref[...] = jnp.zeros_like(totals_ref)
        wait_all(once)

    def body(items, group, slot):
        probe = halves((probe_ref[:, :extent], probe_ref[:, extent:]))
        fields = [(back_ref[at, 0], back_ref[at, 1]) for at in items]
        for at, grad in zip(items, inverse(fields, tables_of(tabs))):
            add_window(
                totals_ref, meta_ref[3 * K + at], meta_ref[2 * K + at],
                [product_conj(p, q) for p, q in zip(probe, halves(grad))],
            )

    group_loop(meta_ref, ready, body)
    give_lower(totals_ref, lower_ref)


MIB = 1024 * 1024
VMEM = 60 * MIB
LIMIT = 46 * MIB


smem = pl.BlockSpec(memory_space=pltpu.SMEM)
vmem = pl.BlockSpec(memory_space=pltpu.VMEM)
hbm = pl.BlockSpec(memory_space=pltpu.HBM)
anywhere = pl.BlockSpec(memory_space=pl.ANY)


def call(kernel, name, ins, in_specs, outs, out_specs, scratch, estimate=None, limit=VMEM):
    return pl.pallas_call(
        kernel,
        in_specs=in_specs,
        out_specs=out_specs,
        out_shape=outs,
        scratch_shapes=scratch,
        compiler_params=pltpu.CompilerParams(vmem_limit_bytes=limit),
        cost_estimate=estimate,
        name=name,
    )(*ins)


def cost(transforms, extent):
    return pl.CostEstimate(
        flops=int(K * transforms * 8 * 2 * extent**3), bytes_accessed=0, transcendentals=0
    )


def sems(*shape):
    return pltpu.SemaphoreType.DMA(shape)


def like(x):
    return pltpu.VMEM(x.shape, x.dtype)


def route(images, here, owner_tile, row_offset, col_offset, permute, tiles):
    reads, extent = images.shape[:2]
    outs = [
        pltpu.HBM((CAP * tiles, extent, extent), bf16),
        jax.ShapeDtypeStruct((4 * K + 8,), jnp.int32),
    ]
    numbers = pltpu.SMEM(owner_tile.shape, jnp.int32)
    scratch = [
        numbers, numbers, numbers, pltpu.SMEM((K + 8,), jnp.int32),
        like(images), like(permute), like(images), like(images), sems(4), sems(reads), sems(reads),
    ]
    ins = [here, owner_tile, row_offset, col_offset, images, permute]
    return call(route_kernel, "route", ins, [smem] + [hbm] * 5, outs, [hbm, smem], scratch, cost(0.25, extent))


def shards_scratch(rows, slabs):
    return pltpu.VMEM((2, slabs) + rows[0].shape[-4:], bf16)


def rows_padded(rows, slabs):
    planes, blocks, height, _ = rows[0].shape[-4:]
    return pltpu.VMEM((planes, blocks, 2 * slabs * height, COLS), f32)


def groups(extent, dtype):
    return pltpu.HBM((K // GROUP, GROUP, 2, extent, extent), dtype)


def group_buffer(extent, dtype):
    return pltpu.VMEM((2, GROUP, 2, extent, extent), dtype)


def waves(meta, rows, probe, kernel, tabs, slabs):
    extent = probe.shape[0]
    scratch = [
        shards_scratch(rows, slabs), like(probe), like(kernel), like(tabs), rows_padded(rows, slabs),
        group_buffer(extent, f32), sems(2 * slabs + 3), sems(2, 1),
    ]
    return call(
        functools.partial(wave_kernel, len(rows)), "waves", [meta] + rows + [probe, kernel, tabs],
        [smem] + [anywhere] * len(rows) + [hbm] * 3, groups(extent, f32), hbm, scratch,
        cost(2, extent),
    )


def totals_out(extent, blocks):
    return [
        pltpu.VMEM((2, blocks, 3 * extent, COLS), f32),
        jax.ShapeDtypeStruct((2, blocks, extent, COLS), bf16),
    ]


def misfits(meta, rows, wave, images, tabs, slabs):
    extent = images.shape[1]
    scratch = [
        shards_scratch(rows, slabs), like(tabs), rows_padded(rows, slabs),
        group_buffer(extent, f32), pltpu.VMEM((2, GROUP, extent, extent), bf16),
        sems(2 * slabs + 1), sems(2, 1 + GROUP),
    ]
    return call(
        functools.partial(misfit_kernel, len(rows)), "misfits", [meta] + rows + [wave, images, tabs],
        [smem] + [anywhere] * len(rows) + [hbm, anywhere, hbm],
        [pltpu.VMEM((K, 2, extent, extent), bf16)] + totals_out(extent, rows[0].shape[-3]), [vmem, vmem, vmem],
        scratch, cost(2, extent), limit=LIMIT,
    )


def backs(meta, fields, kernel, tabs):
    extent = kernel.shape[1]
    return call(
        back_kernel, "backs", [meta, fields, kernel, tabs], [smem, vmem, hbm, hbm],
        pltpu.VMEM((K, 2, extent, extent), bf16), vmem, [like(kernel), like(tabs), sems(2)],
        cost(1, extent), limit=30 * MIB,
    )


def exits(meta, back, probe, tabs, blocks):
    extent = probe.shape[0]
    return call(
        exit_kernel, "exits", [meta, back, probe, tabs], [smem, vmem, hbm, hbm], totals_out(extent, blocks),
        [vmem, vmem], [like(probe), like(tabs), sems(2)], cost(0.1, extent), limit=30 * MIB,
    )


def combine(here, own, moved, count):
    shape = own.shape[:2] + (moved.shape[2] // count, COLS)
    outs = [jax.ShapeDtypeStruct(shape, f32 if k == 0 else bf16) for k in range(count)]
    return call(combine_kernel, "combine", [here, own, moved], [smem, vmem, vmem], outs, [vmem] * count, [], limit=VMEM // 4)


def finish(parts, count):
    blocks, height = parts[0].shape[1:3]
    out = jax.ShapeDtypeStruct((len(parts) // count, 2, height, blocks * COLS), f32)
    return call(
        functools.partial(finish_kernel, count), "finish", parts, [vmem] * len(parts), out, vmem, [], limit=VMEM // 4
    )


def passed_along(value, axis, steps):
    count = lax.axis_size(axis)
    pairs = [(source, (source + steps) % count) for source in range(count)]
    return lax.ppermute(value, axis, pairs)


def shards(intensities, object_field, probe_wave, owner_tile, row_offset, col_offset):
    tile_count = lax.axis_size("tile")
    slab_count = lax.axis_size("slab")
    extent = intensities.shape[1]
    depth, _, height, width = object_field.shape
    blocks = width // COLS
    tabs, kernel, permute = make_tables(extent)
    here = jnp.stack(
        [lax.axis_index("tile"), lax.axis_index("slab"), jnp.int32(slab_count)]
    ).astype(jnp.int32)
    own = jnp.transpose(
        object_field.reshape(depth, 2, height, blocks, COLS), (0, 1, 3, 2, 4)
    ).astype(bf16)
    tabs = jnp.stack(tabs)
    following = passed_along(own, "tile", -1)
    packed, meta = route(
        intensities, here, owner_tile, row_offset, col_offset,
        jnp.stack([permute, permute.T]), tile_count,
    )
    def gather(rows):
        return [rows] + [passed_along(rows, "slab", k) for k in range(1, slab_count)]

    mine0 = gather(own[0])
    packed, following, *mine0 = lax.optimization_barrier((packed, following, *mine0))
    images = lax.all_to_all(packed, "tile", split_axis=0, concat_axis=0, tiled=True)
    next0 = gather(following[0])
    second = gather(jnp.stack([own[1], following[1]]))
    first = mine0 + next0
    wave = waves(meta, first, probe_wave, kernel, tabs, slab_count)
    fields, total1, lower1 = misfits(meta, second, wave, images, tabs, slab_count)
    moved1 = passed_along(lower1, "tile", 1)
    back = backs(meta, fields, kernel, tabs)
    mine1, *sends1 = combine(here, total1, moved1, slab_count)
    total0, lower0 = exits(meta, back, probe_wave, tabs, blocks)
    lower0, mine1, *sends1 = lax.optimization_barrier((lower0, mine1, *sends1))
    moved0 = passed_along(lower0, "tile", 1)
    parts1 = [mine1] + [passed_along(x, "slab", k + 1) for k, x in enumerate(sends1)]
    mine0, *sends0 = combine(here, total0, moved0, slab_count)
    parts0 = [mine0] + [passed_along(x, "slab", k + 1) for k, x in enumerate(sends0)]
    return finish(parts0 + parts1, slab_count)


def solution(mesh):
    placed = (
        P(("tile", "slab"), None, None),
        P(None, None, ("tile", "slab"), None),
        P(),
        P(),
        P(),
        P(),
    )
    return jax.shard_map(
        shards,
        mesh=mesh,
        in_specs=placed,
        out_specs=P(None, None, ("tile", "slab"), None),
        check_vma=False,
    )
```

```python
import functools
import math

import jax
import jax.numpy as jnp
import ml_dtypes
import numpy as np
from jax import lax
from jax.experimental import pallas as pl
from jax.experimental.pallas import tpu as pltpu
from jax.sharding import PartitionSpec as P

K = 16
CAP = 2
GROUP = 4
WIDE = 8
CHUNK = 64
COLS = 128
chirp_strength = 40.0
bf16 = jnp.bfloat16
f32 = jnp.float32


def make_tables(extent):
    counter = np.arange(extent, dtype=np.int64)
    angles = (counter[:, None] * counter[None, :] % extent).astype(np.float32) * np.float32(
        2.0 * math.pi / extent
    )
    scaling = np.float32(1.0 / math.sqrt(extent))
    cosine = (np.cos(angles) * scaling).astype(ml_dtypes.bfloat16)
    sine_part = (np.sin(angles) * scaling).astype(ml_dtypes.bfloat16)
    half = extent // 2
    tables = []
    for parity in (0, 1):
        c, s = cosine[:half, parity::2], sine_part[:half, parity::2]
        table = np.concatenate([np.concatenate([c, -s], 1), np.concatenate([s, c], 1)], 0)
        tables += [table, np.ascontiguousarray(table.T)]
    order = np.concatenate([counter[0::2], counter[1::2]])
    frequency = (((counter + half) % extent - half).astype(np.float32) / extent)[order]
    phases = np.float32(chirp_strength) * (frequency[:, None] ** 2 + frequency[None, :] ** 2)
    kernel = np.stack([np.cos(phases), -np.sin(phases)]).astype(np.float32)
    permute = (counter[:, None] == order[None, :]).astype(ml_dtypes.bfloat16)
    return [jnp.asarray(t) for t in tables], jnp.asarray(kernel), jnp.asarray(permute)


def dot(a, b):
    return jnp.dot(a, b, preferred_element_type=f32)


def row_dot(fields, table):
    n = fields[0].shape[0]
    out = dot(jnp.concatenate(fields, 0), table)
    return [out[i * n : (i + 1) * n] for i in range(len(fields))]


def quads(a, b, h):
    return jnp.concatenate(
        [
            jnp.concatenate([a[:, :h], b[:, :h]], 1),
            jnp.concatenate([a[:, h:], b[:, h:]], 1),
        ],
        0,
    )


def folded(field):
    l, r = field
    return (
        jnp.concatenate([l[0] + r[0], l[1] + r[1]], 1).astype(bf16),
        jnp.concatenate([l[0] - r[0], l[1] - r[1]], 1).astype(bf16),
    )


def forward(items, tabs):
    a_even, t_even, a_odd, t_odd = tabs
    h = a_even.shape[0] // 2
    even = row_dot([x[0] for x in items], a_even)
    odd = row_dot([x[1] for x in items], a_odd)
    plus = [quads(a[:h] + a[h:], b[:h] + b[h:], h).astype(bf16) for a, b in zip(even, odd)]
    minus = [quads(a[:h] - a[h:], b[:h] - b[h:], h).astype(bf16) for a, b in zip(even, odd)]
    return list(zip([dot(t_even, x) for x in plus], [dot(t_odd, x) for x in minus]))


def inverse(items, tabs):
    a_even, t_even, a_odd, t_odd = tabs
    h = a_even.shape[0] // 2

    def side(x, k):
        lanes = slice(k * h, (k + 1) * h)
        return jnp.concatenate(
            [jnp.concatenate([part[:h, lanes], part[h:, lanes]], 1) for part in x], 0
        )

    even = row_dot([side(x, 0) for x in items], t_even)
    odd = row_dot([side(x, 1) for x in items], t_odd)
    plus = [a + b for a, b in zip(even, odd)]
    minus = [a - b for a, b in zip(even, odd)]
    low = [dot(a_even, quads(a[:h], b[:h], h).astype(bf16)) for a, b in zip(plus, minus)]
    high = [dot(a_odd, quads(a[h:], b[h:], h).astype(bf16)) for a, b in zip(plus, minus)]
    out = []
    for a, b in zip(low, high):
        s, d = a + b, a - b
        out.append(
            (jnp.concatenate([s[:h], d[:h]], 0), jnp.concatenate([s[h:], d[h:]], 0))
        )
    return out


def product(a, b):
    return a[0] * b[0] - a[1] * b[1], a[0] * b[1] + a[1] * b[0]


def product_conj(a, b):
    return a[0] * b[0] + a[1] * b[1], a[0] * b[1] - a[1] * b[0]


def halves(x, h=COLS):
    return (x[0][:, :h], x[1][:, :h]), (x[0][:, h:], x[1][:, h:])


def by_kernel(field, kernel_ref, conjugate):
    out = []
    h = field[0].shape[0] // 2
    op = product_conj if conjugate else product
    for k, part in enumerate(field):
        rows = slice(k * h, (k + 1) * h)
        spread = op((kernel_ref[0, rows, :], kernel_ref[1, rows, :]), (part[:h], part[h:]))
        out.append(jnp.concatenate(spread, 0).astype(bf16))
    return out


def window(rows_ref, top, col, extent):
    return tuple(
        tuple(rows_ref[plane, col + j, pl.ds(top, extent), :] for plane in (0, 1)) for j in (0, 1)
    )


def start_all(copies):
    for copy in copies:
        copy.start()
    return copies


def wait_all(copies):
    for copy in copies:
        copy.wait()


def copies_of(pairs, sems):
    return [pltpu.make_async_copy(a, b, sems.at[i]) for i, (a, b) in enumerate(pairs)]


def shard_copies(refs, shards):
    count = shards.shape[1]
    if len(refs) == count:
        return [(ref.at[side], shards.at[side, k]) for k, ref in enumerate(refs) for side in (0, 1)]
    return [(ref, shards.at[i // count, i % count]) for i, ref in enumerate(refs)]


def load_rows(slab_here, shards, rows_ref):
    count = shards.shape[1]
    height = shards.shape[-2]
    for side in (0, 1):
        for k in range(count):
            place = lax.rem(slab_here + count - k, count)
            start = pl.multiple_of((side * count + place) * height, height)
            rows_ref[:, :, pl.ds(start, height), :] = shards[side, k].astype(f32)


def group_count(meta_ref, size):
    return lax.div(meta_ref[4 * K] + size - 1, size)


def group_loop(meta_ref, ready, body, incoming=None, outgoing=None, size=GROUP):
    last = group_count(meta_ref, size)

    def each(make, group, do):
        if make is not None:
            for copy in make(group, lax.rem(group, 2)):
                do(copy)

    @pl.when(last > 0)
    def _():
        each(incoming, 0, lambda c: c.start())

    ready()

    def step(group, carry):
        @pl.when(group + 1 < last)
        def _():
            each(incoming, group + 1, lambda c: c.start())

        each(incoming, group, lambda c: c.wait())

        @pl.when(group >= 2)
        def _():
            each(outgoing, group - 2, lambda c: c.wait())

        body([size * group + j for j in range(size)], group, lax.rem(group, 2))
        each(outgoing, group, lambda c: c.start())
        return carry

    lax.fori_loop(0, last, step, 0)
    for back in (2, 1):

        @pl.when(last >= back)
        def _():
            each(outgoing, last - back, lambda c: c.wait())


def rows_of(field, start, count):
    return tuple(tuple(part[start : start + count] for part in side) for side in field)


def add_window(totals_ref, top, col, term, start=0):
    count = term[0][0].shape[0]
    for j in (0, 1):
        for plane in (0, 1):
            place = (plane, col + j, pl.ds(top + start, count), slice(None))
            totals_ref[place] += term[j][plane]


def route_kernel(
    here_ref, owner_hbm, row_hbm, col_hbm, images_hbm, permute_hbm, out_hbm, meta_ref,
    owner_ref, row_ref, col_ref, second_ref, images_ref, permute_ref, turned_ref, packed_ref,
    sems, in_sems, out_sems,
):
    reads, extent, _ = images_ref.shape
    tiles = out_hbm.shape[0] // CAP
    tile_here, slab_here, slabs = here_ref[0], here_ref[1], here_ref[2]
    mine = (tile_here * slabs + slab_here) * reads
    small = copies_of(
        [(owner_hbm, owner_ref), (row_hbm, row_ref), (col_hbm, col_ref), (permute_hbm, permute_ref)], sems
    )
    start_all(small)
    arriving = copies_of([(images_hbm.at[i], images_ref.at[i]) for i in range(reads)], in_sems)
    start_all(arriving)
    wait_all(small)
    owners = [owner_ref[mine + i] for i in range(reads)]
    leaving = []
    for group in (range(reads // 2), range(reads // 2, reads)):
        for i in group:
            arriving[i].wait()
        for i in group:
            turned_ref[i] = dot(images_ref[i], permute_ref[0]).astype(bf16)
        for i in group:
            packed_ref[i] = dot(permute_ref[1], turned_ref[i]).astype(bf16)
        for i in group:
            rank = jnp.int32(0)
            for j in range(i):
                rank += (owners[j] == owners[i]).astype(jnp.int32)
            copy = pltpu.make_async_copy(
                packed_ref.at[i], out_hbm.at[owners[i] * CAP + rank], out_sems.at[i]
            )
            copy.start()
            leaving.append(copy)

    def sender(g, counts):
        base = (g * slabs + slab_here) * reads
        first, later = counts
        seen = jnp.int32(0)
        for i in range(reads):
            match = (owner_ref[base + i] == tile_here).astype(jnp.int32)
            meta_ref[first] = base + i
            second_ref[later] = base + i
            fresh = match * (1 - seen)
            first, later, seen = first + fresh, later + match - fresh, seen + match
        return first, later

    first, later = lax.fori_loop(0, tiles, sender, (jnp.int32(0), jnp.int32(0)))
    total = first + later
    for i in range(K):
        in_first = i < first
        live = i < total
        row = jnp.where(in_first, meta_ref[i], second_ref[jnp.maximum(i - first, 0)])
        row = jnp.where(live, row, 0)
        group = row // (slabs * reads)
        meta_ref[i] = group * CAP + jnp.where(in_first, 0, 1)
        meta_ref[K + i] = row_ref[row]
        meta_ref[2 * K + i] = col_ref[row]
        meta_ref[3 * K + i] = jnp.where(live, row_ref[row], 2 * extent)
    meta_ref[4 * K] = total
    meta_ref[4 * K + 1] = first
    meta_ref[4 * K + 2] = slab_here
    wait_all(leaving)


def give_lower(totals_ref, lower_ref):
    rows = lower_ref.shape[2]
    lower_ref[...] = totals_ref[:, :, rows : 2 * rows, :].astype(bf16)


def combine_kernel(here_ref, own_ref, moved_ref, mine_ref, *send_refs):
    height = mine_ref.shape[2]
    count = len(send_refs) + 1
    for k in range(count):
        place = lax.rem(here_ref[1] + k, count)
        rows = pl.ds(pl.multiple_of(place * height, height), height)
        both = own_ref[:, :, rows, :] + moved_ref[:, :, rows, :].astype(f32)
        if k == 0:
            mine_ref[...] = both
        else:
            send_refs[k - 1][...] = both.astype(bf16)


def finish_kernel(count, *refs):
    out_ref = refs[-1]
    for s in range(out_ref.shape[0]):
        parts = refs[s * count : (s + 1) * count]
        for plane in (0, 1):
            for block in range(parts[0].shape[1]):
                total = parts[0][plane, block]
                for part in parts[1:]:
                    total = total + part[plane, block].astype(f32)
                out_ref[s, plane, :, block * COLS : (block + 1) * COLS] = total


def tables_of(tabs_ref):
    return tuple(tabs_ref[i] for i in range(4))


def wave_kernel(count, meta_ref, *refs):
    rows_hbm = refs[:count]
    (probe_hbm, kernel_hbm, tabs_hbm, wave_hbm,
     shards, probe_ref, kernel_ref, tabs, rows_ref, wave_buf, sems, out_sems) = refs[count:]
    extent = probe_ref.shape[0]
    once = start_all(copies_of(
        shard_copies(rows_hbm, shards)
        + [(probe_hbm, probe_ref), (kernel_hbm, kernel_ref), (tabs_hbm, tabs)], sems))

    def ready():
        wait_all(once)
        load_rows(meta_ref[4 * K + 2], shards, rows_ref)

    def outgoing(group, slot):
        return copies_of([(wave_buf.at[slot], wave_hbm.at[group])], out_sems.at[slot])

    def body(items, group, slot):
        tables = tables_of(tabs)
        probe = halves((probe_ref[:, :extent], probe_ref[:, extent:]))
        fields = []
        for at in items:
            w = window(rows_ref, meta_ref[K + at], meta_ref[2 * K + at], extent)
            fields.append(folded(tuple(product(p, q) for p, q in zip(probe, w))))
        spread = [by_kernel(x, kernel_ref, False) for x in forward(fields, tables)]
        for i, wave in enumerate(inverse(spread, tables)):
            wave_buf[slot, i, 0] = wave[0]
            wave_buf[slot, i, 1] = wave[1]

    group_loop(meta_ref, ready, body, None, outgoing)


def misfit_kernel(count, meta_ref, *refs):
    rows_hbm = refs[:count]
    (wave_hbm, images_hbm, tabs_hbm, back_ref, totals_ref, lower_ref,
     shards, tabs, rows_ref, wave_buf, image_buf, sems, in_sems) = refs[count:]
    extent = images_hbm.shape[1]
    h = extent // 2
    once = start_all(copies_of(shard_copies(rows_hbm, shards) + [(tabs_hbm, tabs)], sems))

    def ready():
        totals_ref[...] = jnp.zeros_like(totals_ref)
        wait_all(once)
        load_rows(meta_ref[4 * K + 2], shards, rows_ref)

    def incoming(group, slot):
        return copies_of(
            [(wave_hbm.at[group], wave_buf.at[slot])]
            + [(images_hbm.at[meta_ref[GROUP * group + i]], image_buf.at[slot, i]) for i in range(GROUP)],
            in_sems.at[slot],
        )

    def body(items, group, slot):
        tables = tables_of(tabs)

        def wave_of(i):
            return halves((wave_buf[slot, i, 0], wave_buf[slot, i, 1]))

        fields = []
        for i, at in enumerate(items):
            w = window(rows_ref, meta_ref[K + at], meta_ref[2 * K + at], extent)
            fields.append(folded(tuple(product(p, q) for p, q in zip(wave_of(i), w))))
        far_grads = []
        for i, far in enumerate(forward(fields, tables)):
            parts = []
            for k, part in enumerate(far):
                re, im = part[:h], part[h:]
                image = image_buf[slot, i, k * h : (k + 1) * h, :].astype(f32)
                misfit = re * re + im * im - image
                parts.append(jnp.concatenate([re * misfit, im * misfit], 0).astype(bf16))
            far_grads.append(parts)
        for i, (at, grad) in enumerate(zip(items, inverse(far_grads, tables))):
            grad = halves(grad)
            top, col = meta_ref[K + at], meta_ref[2 * K + at]
            target = meta_ref[3 * K + at]
            for start in range(0, extent, CHUNK):
                rows = slice(start, start + CHUNK)
                part = rows_of(grad, start, CHUNK)
                wave = halves((wave_buf[slot, i, 0, rows], wave_buf[slot, i, 1, rows]))
                term = [product_conj(p, q) for p, q in zip(wave, part)]
                add_window(totals_ref, target, col, term, start)
                w = window(rows_ref, top + start, col, CHUNK)
                back = folded(tuple(product_conj(p, q) for p, q in zip(w, part)))
                for k in (0, 1):
                    back_ref[at, k, rows] = back[k]

    group_loop(meta_ref, ready, body, incoming)
    give_lower(totals_ref, lower_ref)


def exit_kernel(
    meta_ref, fields_ref, probe_hbm, kernel_hbm, tabs_hbm, totals_ref, lower_ref, probe_ref, kernel_ref, tabs, sems
):
    extent = probe_ref.shape[0]
    once = start_all(copies_of([(probe_hbm, probe_ref), (kernel_hbm, kernel_ref), (tabs_hbm, tabs)], sems))

    def ready():
        totals_ref[...] = jnp.zeros_like(totals_ref)
        wait_all(once)

    def body(items, group, slot):
        tables = tables_of(tabs)
        fields = [(fields_ref[at, 0], fields_ref[at, 1]) for at in items]
        back = [by_kernel(x, kernel_ref, True) for x in forward(fields, tables)]
        grads = [halves(x) for x in inverse(back, tables)]
        for start in range(0, extent, CHUNK):
            rows = slice(start, start + CHUNK)
            probe = halves((probe_ref[rows, :extent], probe_ref[rows, extent:]))
            for at, grad in zip(items, grads):
                term = [product_conj(p, q) for p, q in zip(probe, rows_of(grad, start, CHUNK))]
                add_window(totals_ref, meta_ref[3 * K + at], meta_ref[2 * K + at], term, start)

    group_loop(meta_ref, ready, body, size=WIDE)
    give_lower(totals_ref, lower_ref)


MIB = 1024 * 1024
VMEM = 60 * MIB
LIMIT = 46 * MIB


smem = pl.BlockSpec(memory_space=pltpu.SMEM)
vmem = pl.BlockSpec(memory_space=pltpu.VMEM)
hbm = pl.BlockSpec(memory_space=pltpu.HBM)
anywhere = pl.BlockSpec(memory_space=pl.ANY)


def call(kernel, name, ins, in_specs, outs, out_specs, scratch, estimate=None, limit=VMEM):
    return pl.pallas_call(
        kernel,
        in_specs=in_specs,
        out_specs=out_specs,
        out_shape=outs,
        scratch_shapes=scratch,
        compiler_params=pltpu.CompilerParams(vmem_limit_bytes=limit),
        cost_estimate=estimate,
        name=name,
    )(*ins)


def cost(transforms, extent):
    return pl.CostEstimate(
        flops=int(K * transforms * 8 * 2 * extent**3), bytes_accessed=0, transcendentals=0
    )


def sems(*shape):
    return pltpu.SemaphoreType.DMA(shape)


def like(x):
    return pltpu.VMEM(x.shape, x.dtype)


def route(images, here, owner_tile, row_offset, col_offset, permute, tiles):
    reads, extent = images.shape[:2]
    outs = [
        pltpu.HBM((CAP * tiles, extent, extent), bf16),
        jax.ShapeDtypeStruct((4 * K + 8,), jnp.int32),
    ]
    numbers = pltpu.SMEM(owner_tile.shape, jnp.int32)
    scratch = [
        numbers, numbers, numbers, pltpu.SMEM((K + 8,), jnp.int32),
        like(images), like(permute), like(images), like(images), sems(4), sems(reads), sems(reads),
    ]
    ins = [here, owner_tile, row_offset, col_offset, images, permute]
    return call(route_kernel, "route", ins, [smem] + [hbm] * 5, outs, [hbm, smem], scratch, cost(0.25, extent))


def shards_scratch(rows, slabs):
    return pltpu.VMEM((2, slabs) + rows[0].shape[-4:], bf16)


def rows_padded(rows, slabs):
    planes, blocks, height, _ = rows[0].shape[-4:]
    return pltpu.VMEM((planes, blocks, 2 * slabs * height, COLS), f32)


def groups(extent, dtype):
    return pltpu.HBM((K // GROUP, GROUP, 2, extent, extent), dtype)


def group_buffer(extent, dtype):
    return pltpu.VMEM((2, GROUP, 2, extent, extent), dtype)


def waves(meta, rows, probe, kernel, tabs, slabs):
    extent = probe.shape[0]
    scratch = [
        shards_scratch(rows, slabs), like(probe), like(kernel), like(tabs), rows_padded(rows, slabs),
        group_buffer(extent, f32), sems(2 * slabs + 3), sems(2, 1),
    ]
    return call(
        functools.partial(wave_kernel, len(rows)), "waves", [meta] + rows + [probe, kernel, tabs],
        [smem] + [anywhere] * len(rows) + [hbm] * 3, groups(extent, f32), hbm, scratch,
        cost(2, extent),
    )


def totals_out(extent, blocks):
    return [
        pltpu.VMEM((2, blocks, 3 * extent, COLS), f32),
        jax.ShapeDtypeStruct((2, blocks, extent, COLS), bf16),
    ]


def misfits(meta, rows, wave, images, tabs, slabs):
    extent = images.shape[1]
    scratch = [
        shards_scratch(rows, slabs), like(tabs), rows_padded(rows, slabs),
        group_buffer(extent, f32), pltpu.VMEM((2, GROUP, extent, extent), bf16),
        sems(2 * slabs + 1), sems(2, 1 + GROUP),
    ]
    return call(
        functools.partial(misfit_kernel, len(rows)), "misfits", [meta] + rows + [wave, images, tabs],
        [smem] + [anywhere] * len(rows) + [hbm, anywhere, hbm],
        [pltpu.VMEM((K, 2, extent, extent), bf16)] + totals_out(extent, rows[0].shape[-3]), [vmem, vmem, vmem],
        scratch, cost(2, extent), limit=LIMIT,
    )


def exits(meta, fields, probe, kernel, tabs, blocks):
    extent = probe.shape[0]
    return call(
        exit_kernel, "exits", [meta, fields, probe, kernel, tabs], [smem, vmem, hbm, hbm, hbm],
        totals_out(extent, blocks), [vmem, vmem], [like(probe), like(kernel), like(tabs), sems(3)],
        cost(0.1, extent), limit=30 * MIB,
    )


def combine(here, own, moved, count):
    shape = own.shape[:2] + (moved.shape[2] // count, COLS)
    outs = [jax.ShapeDtypeStruct(shape, f32 if k == 0 else bf16) for k in range(count)]
    return call(combine_kernel, "combine", [here, own, moved], [smem, vmem, vmem], outs, [vmem] * count, [], limit=VMEM // 4)


def finish(parts, count):
    blocks, height = parts[0].shape[1:3]
    out = jax.ShapeDtypeStruct((len(parts) // count, 2, height, blocks * COLS), f32)
    return call(
        functools.partial(finish_kernel, count), "finish", parts, [vmem] * len(parts), out, vmem, [], limit=VMEM // 4
    )


def passed_along(value, axis, steps):
    count = lax.axis_size(axis)
    pairs = [(source, (source + steps) % count) for source in range(count)]
    return lax.ppermute(value, axis, pairs)


def shards(intensities, object_field, probe_wave, owner_tile, row_offset, col_offset):
    tile_count = lax.axis_size("tile")
    slab_count = lax.axis_size("slab")
    extent = intensities.shape[1]
    depth, _, height, width = object_field.shape
    blocks = width // COLS
    tabs, kernel, permute = make_tables(extent)
    here = jnp.stack(
        [lax.axis_index("tile"), lax.axis_index("slab"), jnp.int32(slab_count)]
    ).astype(jnp.int32)
    own = jnp.transpose(
        object_field.reshape(depth, 2, height, blocks, COLS), (0, 1, 3, 2, 4)
    ).astype(bf16)
    tabs = jnp.stack(tabs)
    following = passed_along(own, "tile", -1)
    packed, meta = route(
        intensities, here, owner_tile, row_offset, col_offset,
        jnp.stack([permute, permute.T]), tile_count,
    )
    def gather(rows):
        return [rows] + [passed_along(rows, "slab", k) for k in range(1, slab_count)]

    mine0 = gather(own[0])
    packed, following, *mine0 = lax.optimization_barrier((packed, following, *mine0))
    images = lax.all_to_all(packed, "tile", split_axis=0, concat_axis=0, tiled=True)
    next0 = gather(following[0])
    second = gather(jnp.stack([own[1], following[1]]))
    first = mine0 + next0
    wave = waves(meta, first, probe_wave, kernel, tabs, slab_count)
    fields, total1, lower1 = misfits(meta, second, wave, images, tabs, slab_count)
    moved1 = passed_along(lower1, "tile", 1)
    mine1, *sends1 = combine(here, total1, moved1, slab_count)
    total0, lower0 = exits(meta, fields, probe_wave, kernel, tabs, blocks)
    lower0, mine1, *sends1 = lax.optimization_barrier((lower0, mine1, *sends1))
    moved0 = passed_along(lower0, "tile", 1)
    parts1 = [mine1] + [passed_along(x, "slab", k + 1) for k, x in enumerate(sends1)]
    mine0, *sends0 = combine(here, total0, moved0, slab_count)
    parts0 = [mine0] + [passed_along(x, "slab", k + 1) for k, x in enumerate(sends0)]
    return finish(parts0 + parts1, slab_count)


def solution(mesh):
    placed = (
        P(("tile", "slab"), None, None),
        P(None, None, ("tile", "slab"), None),
        P(),
        P(),
        P(),
        P(),
    )
    return jax.shard_map(
        shards,
        mesh=mesh,
        in_specs=placed,
        out_specs=P(None, None, ("tile", "slab"), None),
        check_vma=False,
    )
```

```python
import functools
import math

import jax
import jax.numpy as jnp
import ml_dtypes
import numpy as np
from jax import lax
from jax.experimental import pallas as pl
from jax.experimental.pallas import tpu as pltpu
from jax.sharding import PartitionSpec as P

K = 16
CAP = 2
GROUP = 4
WIDE = 8
CHUNK = 64
COLS = 128
chirp_strength = 40.0
bf16 = jnp.bfloat16
f32 = jnp.float32


def make_tables(extent):
    counter = np.arange(extent, dtype=np.int64)
    angles = (counter[:, None] * counter[None, :] % extent).astype(np.float32) * np.float32(
        2.0 * math.pi / extent
    )
    scaling = np.float32(1.0 / math.sqrt(extent))
    cosine = (np.cos(angles) * scaling).astype(ml_dtypes.bfloat16)
    sine_part = (np.sin(angles) * scaling).astype(ml_dtypes.bfloat16)
    half = extent // 2
    tables = []
    for parity in (0, 1):
        c, s = cosine[:half, parity::2], sine_part[:half, parity::2]
        table = np.concatenate([np.concatenate([c, -s], 1), np.concatenate([s, c], 1)], 0)
        tables += [table, np.ascontiguousarray(table.T)]
    order = np.concatenate([counter[0::2], counter[1::2]])
    frequency = (((counter + half) % extent - half).astype(np.float32) / extent)[order]
    phases = np.float32(chirp_strength) * (frequency[:, None] ** 2 + frequency[None, :] ** 2)
    kernel = np.stack([np.cos(phases), -np.sin(phases)]).astype(np.float32)
    permute = (counter[:, None] == order[None, :]).astype(ml_dtypes.bfloat16)
    return [jnp.asarray(t) for t in tables], jnp.asarray(kernel), jnp.asarray(permute)


def dot(a, b):
    return jnp.dot(a, b, preferred_element_type=f32)


def row_dot(fields, table):
    n = fields[0].shape[0]
    out = dot(jnp.concatenate(fields, 0), table)
    return [out[i * n : (i + 1) * n] for i in range(len(fields))]


def quads(a, b, h):
    return jnp.concatenate(
        [
            jnp.concatenate([a[:, :h], b[:, :h]], 1),
            jnp.concatenate([a[:, h:], b[:, h:]], 1),
        ],
        0,
    )


def folded(field):
    l, r = field
    return (
        jnp.concatenate([l[0] + r[0], l[1] + r[1]], 1).astype(bf16),
        jnp.concatenate([l[0] - r[0], l[1] - r[1]], 1).astype(bf16),
    )


def forward(items, tabs):
    a_even, t_even, a_odd, t_odd = tabs
    h = a_even.shape[0] // 2
    even = row_dot([x[0] for x in items], a_even)
    odd = row_dot([x[1] for x in items], a_odd)
    plus = [quads(a[:h] + a[h:], b[:h] + b[h:], h).astype(bf16) for a, b in zip(even, odd)]
    minus = [quads(a[:h] - a[h:], b[:h] - b[h:], h).astype(bf16) for a, b in zip(even, odd)]
    return list(zip([dot(t_even, x) for x in plus], [dot(t_odd, x) for x in minus]))


def inverse(items, tabs):
    a_even, t_even, a_odd, t_odd = tabs
    h = a_even.shape[0] // 2

    def side(x, k):
        lanes = slice(k * h, (k + 1) * h)
        return jnp.concatenate(
            [jnp.concatenate([part[:h, lanes], part[h:, lanes]], 1) for part in x], 0
        )

    even = row_dot([side(x, 0) for x in items], t_even)
    odd = row_dot([side(x, 1) for x in items], t_odd)
    plus = [a + b for a, b in zip(even, odd)]
    minus = [a - b for a, b in zip(even, odd)]
    low = [dot(a_even, quads(a[:h], b[:h], h).astype(bf16)) for a, b in zip(plus, minus)]
    high = [dot(a_odd, quads(a[h:], b[h:], h).astype(bf16)) for a, b in zip(plus, minus)]
    out = []
    for a, b in zip(low, high):
        s, d = a + b, a - b
        out.append(
            (jnp.concatenate([s[:h], d[:h]], 0), jnp.concatenate([s[h:], d[h:]], 0))
        )
    return out


def product(a, b):
    return a[0] * b[0] - a[1] * b[1], a[0] * b[1] + a[1] * b[0]


def product_conj(a, b):
    return a[0] * b[0] + a[1] * b[1], a[0] * b[1] - a[1] * b[0]


def cut(x):
    return x[0].astype(bf16), x[1].astype(bf16)


def halves(x, h=COLS):
    return (x[0][:, :h], x[1][:, :h]), (x[0][:, h:], x[1][:, h:])


def by_kernel(field, kernel_ref, conjugate):
    out = []
    h = field[0].shape[0] // 2
    op = product_conj if conjugate else product
    for k, part in enumerate(field):
        rows = slice(k * h, (k + 1) * h)
        spread = op((kernel_ref[0, rows, :], kernel_ref[1, rows, :]), (part[:h], part[h:]))
        out.append(jnp.concatenate(spread, 0).astype(bf16))
    return out


def window(rows_ref, top, col, extent):
    return tuple(
        tuple(rows_ref[plane, col + j, pl.ds(top, extent), :] for plane in (0, 1)) for j in (0, 1)
    )


def start_all(copies):
    for copy in copies:
        copy.start()
    return copies


def wait_all(copies):
    for copy in copies:
        copy.wait()


def copies_of(pairs, sems):
    return [pltpu.make_async_copy(a, b, sems.at[i]) for i, (a, b) in enumerate(pairs)]


def shard_copies(refs, shards):
    count = shards.shape[1]
    if len(refs) == count:
        return [(ref.at[side], shards.at[side, k]) for k, ref in enumerate(refs) for side in (0, 1)]
    return [(ref, shards.at[i // count, i % count]) for i, ref in enumerate(refs)]


def load_rows(slab_here, shards, rows_ref):
    count = shards.shape[1]
    height = shards.shape[-2]
    for side in (0, 1):
        for k in range(count):
            place = lax.rem(slab_here + count - k, count)
            start = pl.multiple_of((side * count + place) * height, height)
            rows_ref[:, :, pl.ds(start, height), :] = shards[side, k].astype(f32)


def group_count(meta_ref, size):
    return lax.div(meta_ref[4 * K] + size - 1, size)


def group_loop(meta_ref, ready, body, incoming=None, outgoing=None, size=GROUP):
    last = group_count(meta_ref, size)

    def each(make, group, do):
        if make is not None:
            for copy in make(group, lax.rem(group, 2)):
                do(copy)

    @pl.when(last > 0)
    def _():
        each(incoming, 0, lambda c: c.start())

    ready()

    def step(group, carry):
        @pl.when(group + 1 < last)
        def _():
            each(incoming, group + 1, lambda c: c.start())

        each(incoming, group, lambda c: c.wait())

        @pl.when(group >= 2)
        def _():
            each(outgoing, group - 2, lambda c: c.wait())

        body([size * group + j for j in range(size)], group, lax.rem(group, 2))
        each(outgoing, group, lambda c: c.start())
        return carry

    lax.fori_loop(0, last, step, 0)
    for back in (2, 1):

        @pl.when(last >= back)
        def _():
            each(outgoing, last - back, lambda c: c.wait())


def rows_of(field, start, count):
    return tuple(tuple(part[start : start + count] for part in side) for side in field)


def add_window(totals_ref, top, col, term, start=0):
    count = term[0][0].shape[0]
    for j in (0, 1):
        for plane in (0, 1):
            place = (plane, col + j, pl.ds(top + start, count), slice(None))
            totals_ref[place] += term[j][plane]


def route_kernel(
    here_ref, owner_hbm, row_hbm, col_hbm, images_hbm, permute_hbm, out_hbm, meta_ref,
    owner_ref, row_ref, col_ref, second_ref, images_ref, permute_ref, turned_ref, packed_ref,
    sems, in_sems, out_sems,
):
    reads, extent, _ = images_ref.shape
    tiles = out_hbm.shape[0] // CAP
    tile_here, slab_here, slabs = here_ref[0], here_ref[1], here_ref[2]
    mine = (tile_here * slabs + slab_here) * reads
    small = copies_of(
        [(owner_hbm, owner_ref), (row_hbm, row_ref), (col_hbm, col_ref), (permute_hbm, permute_ref)], sems
    )
    start_all(small)
    arriving = copies_of([(images_hbm.at[i], images_ref.at[i]) for i in range(reads)], in_sems)
    start_all(arriving)
    wait_all(small)
    owners = [owner_ref[mine + i] for i in range(reads)]
    leaving = []
    for group in (range(reads // 2), range(reads // 2, reads)):
        for i in group:
            arriving[i].wait()
        for i in group:
            turned_ref[i] = dot(images_ref[i], permute_ref[0]).astype(bf16)
        for i in group:
            packed_ref[i] = dot(permute_ref[1], turned_ref[i]).astype(bf16)
        for i in group:
            rank = jnp.int32(0)
            for j in range(i):
                rank += (owners[j] == owners[i]).astype(jnp.int32)
            copy = pltpu.make_async_copy(
                packed_ref.at[i], out_hbm.at[owners[i] * CAP + rank], out_sems.at[i]
            )
            copy.start()
            leaving.append(copy)

    def sender(g, counts):
        base = (g * slabs + slab_here) * reads
        first, later = counts
        seen = jnp.int32(0)
        for i in range(reads):
            match = (owner_ref[base + i] == tile_here).astype(jnp.int32)
            meta_ref[first] = base + i
            second_ref[later] = base + i
            fresh = match * (1 - seen)
            first, later, seen = first + fresh, later + match - fresh, seen + match
        return first, later

    first, later = lax.fori_loop(0, tiles, sender, (jnp.int32(0), jnp.int32(0)))
    total = first + later
    for i in range(K):
        in_first = i < first
        live = i < total
        row = jnp.where(in_first, meta_ref[i], second_ref[jnp.maximum(i - first, 0)])
        row = jnp.where(live, row, 0)
        group = row // (slabs * reads)
        meta_ref[i] = group * CAP + jnp.where(in_first, 0, 1)
        meta_ref[K + i] = row_ref[row]
        meta_ref[2 * K + i] = col_ref[row]
        meta_ref[3 * K + i] = jnp.where(live, row_ref[row], 2 * extent)
    meta_ref[4 * K] = total
    meta_ref[4 * K + 1] = first
    meta_ref[4 * K + 2] = slab_here
    wait_all(leaving)


def give_lower(totals_ref, lower_ref):
    rows = lower_ref.shape[2]
    lower_ref[...] = totals_ref[:, :, rows : 2 * rows, :].astype(bf16)


def combine_kernel(here_ref, own_ref, moved_ref, mine_ref, *send_refs):
    height = mine_ref.shape[2]
    count = len(send_refs) + 1
    for k in range(count):
        place = lax.rem(here_ref[1] + k, count)
        rows = pl.ds(pl.multiple_of(place * height, height), height)
        both = own_ref[:, :, rows, :] + moved_ref[:, :, rows, :].astype(f32)
        if k == 0:
            mine_ref[...] = both
        else:
            send_refs[k - 1][...] = both.astype(bf16)


def finish_kernel(count, *refs):
    out_ref = refs[-1]
    for s in range(out_ref.shape[0]):
        parts = refs[s * count : (s + 1) * count]
        for plane in (0, 1):
            for block in range(parts[0].shape[1]):
                total = parts[0][plane, block]
                for part in parts[1:]:
                    total = total + part[plane, block].astype(f32)
                out_ref[s, plane, :, block * COLS : (block + 1) * COLS] = total


def tables_of(tabs_ref):
    return tuple(tabs_ref[i] for i in range(4))


def wave_kernel(count, meta_ref, *refs):
    rows_hbm = refs[:count]
    (probe_hbm, kernel_hbm, tabs_hbm, wave_hbm,
     shards, probe_ref, kernel_ref, tabs, rows_ref, wave_buf, sems, out_sems) = refs[count:]
    extent = probe_ref.shape[0]
    once = start_all(copies_of(
        shard_copies(rows_hbm, shards)
        + [(probe_hbm, probe_ref), (kernel_hbm, kernel_ref), (tabs_hbm, tabs)], sems))

    def ready():
        wait_all(once)
        load_rows(meta_ref[4 * K + 2], shards, rows_ref)

    def outgoing(group, slot):
        return copies_of([(wave_buf.at[slot], wave_hbm.at[group])], out_sems.at[slot])

    def body(items, group, slot):
        tables = tables_of(tabs)
        probe = [cut(side) for side in halves((probe_ref[:, :extent], probe_ref[:, extent:]))]
        fields = []
        for at in items:
            w = window(rows_ref, meta_ref[K + at], meta_ref[2 * K + at], extent)
            fields.append(folded(tuple(product(p, cut(q)) for p, q in zip(probe, w))))
        spread = [by_kernel(x, kernel_ref, False) for x in forward(fields, tables)]
        for i, wave in enumerate(inverse(spread, tables)):
            wave_buf[slot, i, 0] = wave[0].astype(bf16)
            wave_buf[slot, i, 1] = wave[1].astype(bf16)

    group_loop(meta_ref, ready, body, None, outgoing)


def misfit_kernel(count, meta_ref, *refs):
    rows_hbm = refs[:count]
    (wave_hbm, images_hbm, tabs_hbm, back_ref, totals_ref, lower_ref,
     shards, tabs, rows_ref, wave_buf, image_buf, sems, in_sems) = refs[count:]
    extent = images_hbm.shape[1]
    h = extent // 2
    once = start_all(copies_of(shard_copies(rows_hbm, shards) + [(tabs_hbm, tabs)], sems))

    def ready():
        totals_ref[...] = jnp.zeros_like(totals_ref)
        wait_all(once)
        load_rows(meta_ref[4 * K + 2], shards, rows_ref)

    def incoming(group, slot):
        return copies_of(
            [(wave_hbm.at[group], wave_buf.at[slot])]
            + [(images_hbm.at[meta_ref[GROUP * group + i]], image_buf.at[slot, i]) for i in range(GROUP)],
            in_sems.at[slot],
        )

    def body(items, group, slot):
        tables = tables_of(tabs)

        def wave_of(i):
            return halves((wave_buf[slot, i, 0], wave_buf[slot, i, 1]))

        fields = []
        for i, at in enumerate(items):
            w = window(rows_ref, meta_ref[K + at], meta_ref[2 * K + at], extent)
            fields.append(folded(tuple(product(cut(p), cut(q)) for p, q in zip(wave_of(i), w))))
        far_grads = []
        for i, far in enumerate(forward(fields, tables)):
            parts = []
            for k, part in enumerate(far):
                re, im = part[:h], part[h:]
                image = image_buf[slot, i, k * h : (k + 1) * h, :].astype(f32)
                misfit = re * re + im * im - image
                parts.append(jnp.concatenate([re * misfit, im * misfit], 0).astype(bf16))
            far_grads.append(parts)
        for i, (at, grad) in enumerate(zip(items, inverse(far_grads, tables))):
            grad = halves(grad)
            top, col = meta_ref[K + at], meta_ref[2 * K + at]
            target = meta_ref[3 * K + at]
            for start in range(0, extent, CHUNK):
                rows = slice(start, start + CHUNK)
                part = rows_of(grad, start, CHUNK)
                wave = halves((wave_buf[slot, i, 0, rows].astype(f32), wave_buf[slot, i, 1, rows].astype(f32)))
                term = [product_conj(p, q) for p, q in zip(wave, part)]
                add_window(totals_ref, target, col, term, start)
                w = window(rows_ref, top + start, col, CHUNK)
                back = folded(tuple(product_conj(cut(p), cut(q)) for p, q in zip(w, part)))
                for k in (0, 1):
                    back_ref[at, k, rows] = back[k]

    group_loop(meta_ref, ready, body, incoming)
    give_lower(totals_ref, lower_ref)


def exit_kernel(
    meta_ref, fields_ref, probe_hbm, kernel_hbm, tabs_hbm, totals_ref, lower_ref, probe_ref, kernel_ref, tabs, sems
):
    extent = probe_ref.shape[0]
    once = start_all(copies_of([(probe_hbm, probe_ref), (kernel_hbm, kernel_ref), (tabs_hbm, tabs)], sems))

    def ready():
        totals_ref[...] = jnp.zeros_like(totals_ref)
        wait_all(once)

    def body(items, group, slot):
        tables = tables_of(tabs)
        fields = [(fields_ref[at, 0], fields_ref[at, 1]) for at in items]
        back = [by_kernel(x, kernel_ref, True) for x in forward(fields, tables)]
        grads = [halves(x) for x in inverse(back, tables)]
        for start in range(0, extent, CHUNK):
            rows = slice(start, start + CHUNK)
            probe = halves((probe_ref[rows, :extent], probe_ref[rows, extent:]))
            for at, grad in zip(items, grads):
                term = [product_conj(p, q) for p, q in zip(probe, rows_of(grad, start, CHUNK))]
                add_window(totals_ref, meta_ref[3 * K + at], meta_ref[2 * K + at], term, start)

    group_loop(meta_ref, ready, body, size=WIDE)
    give_lower(totals_ref, lower_ref)


MIB = 1024 * 1024
VMEM = 60 * MIB
LIMIT = 46 * MIB


smem = pl.BlockSpec(memory_space=pltpu.SMEM)
vmem = pl.BlockSpec(memory_space=pltpu.VMEM)
hbm = pl.BlockSpec(memory_space=pltpu.HBM)
anywhere = pl.BlockSpec(memory_space=pl.ANY)


def call(kernel, name, ins, in_specs, outs, out_specs, scratch, estimate=None, limit=VMEM):
    return pl.pallas_call(
        kernel,
        in_specs=in_specs,
        out_specs=out_specs,
        out_shape=outs,
        scratch_shapes=scratch,
        compiler_params=pltpu.CompilerParams(vmem_limit_bytes=limit),
        cost_estimate=estimate,
        name=name,
    )(*ins)


def cost(transforms, extent):
    return pl.CostEstimate(
        flops=int(K * transforms * 8 * 2 * extent**3), bytes_accessed=0, transcendentals=0
    )


def sems(*shape):
    return pltpu.SemaphoreType.DMA(shape)


def like(x):
    return pltpu.VMEM(x.shape, x.dtype)


def route(images, here, owner_tile, row_offset, col_offset, permute, tiles):
    reads, extent = images.shape[:2]
    outs = [
        pltpu.HBM((CAP * tiles, extent, extent), bf16),
        jax.ShapeDtypeStruct((4 * K + 8,), jnp.int32),
    ]
    numbers = pltpu.SMEM(owner_tile.shape, jnp.int32)
    scratch = [
        numbers, numbers, numbers, pltpu.SMEM((K + 8,), jnp.int32),
        like(images), like(permute), like(images), like(images), sems(4), sems(reads), sems(reads),
    ]
    ins = [here, owner_tile, row_offset, col_offset, images, permute]
    return call(route_kernel, "route", ins, [smem] + [hbm] * 5, outs, [hbm, smem], scratch, cost(0.25, extent))


def shards_scratch(rows, slabs):
    return pltpu.VMEM((2, slabs) + rows[0].shape[-4:], bf16)


def rows_padded(rows, slabs):
    planes, blocks, height, _ = rows[0].shape[-4:]
    return pltpu.VMEM((planes, blocks, 2 * slabs * height, COLS), f32)


def groups(extent, dtype):
    return pltpu.HBM((K // GROUP, GROUP, 2, extent, extent), dtype)


def group_buffer(extent, dtype):
    return pltpu.VMEM((2, GROUP, 2, extent, extent), dtype)


def waves(meta, rows, probe, kernel, tabs, slabs):
    extent = probe.shape[0]
    scratch = [
        shards_scratch(rows, slabs), like(probe), like(kernel), like(tabs), rows_padded(rows, slabs),
        group_buffer(extent, bf16), sems(2 * slabs + 3), sems(2, 1),
    ]
    return call(
        functools.partial(wave_kernel, len(rows)), "waves", [meta] + rows + [probe, kernel, tabs],
        [smem] + [anywhere] * len(rows) + [hbm] * 3, groups(extent, bf16), hbm, scratch,
        cost(2, extent),
    )


def totals_out(extent, blocks):
    return [
        pltpu.VMEM((2, blocks, 3 * extent, COLS), f32),
        jax.ShapeDtypeStruct((2, blocks, extent, COLS), bf16),
    ]


def misfits(meta, rows, wave, images, tabs, slabs):
    extent = images.shape[1]
    scratch = [
        shards_scratch(rows, slabs), like(tabs), rows_padded(rows, slabs),
        group_buffer(extent, bf16), pltpu.VMEM((2, GROUP, extent, extent), bf16),
        sems(2 * slabs + 1), sems(2, 1 + GROUP),
    ]
    return call(
        functools.partial(misfit_kernel, len(rows)), "misfits", [meta] + rows + [wave, images, tabs],
        [smem] + [anywhere] * len(rows) + [hbm, anywhere, hbm],
        [pltpu.VMEM((K, 2, extent, extent), bf16)] + totals_out(extent, rows[0].shape[-3]), [vmem, vmem, vmem],
        scratch, cost(2, extent), limit=LIMIT,
    )


def exits(meta, fields, probe, kernel, tabs, blocks):
    extent = probe.shape[0]
    return call(
        exit_kernel, "exits", [meta, fields, probe, kernel, tabs], [smem, vmem, hbm, hbm, hbm],
        totals_out(extent, blocks), [vmem, vmem], [like(probe), like(kernel), like(tabs), sems(3)],
        cost(0.1, extent), limit=30 * MIB,
    )


def combine(here, own, moved, count):
    shape = own.shape[:2] + (moved.shape[2] // count, COLS)
    outs = [jax.ShapeDtypeStruct(shape, f32 if k == 0 else bf16) for k in range(count)]
    return call(combine_kernel, "combine", [here, own, moved], [smem, vmem, vmem], outs, [vmem] * count, [], limit=VMEM // 4)


def finish(parts, count):
    blocks, height = parts[0].shape[1:3]
    out = jax.ShapeDtypeStruct((len(parts) // count, 2, height, blocks * COLS), f32)
    return call(
        functools.partial(finish_kernel, count), "finish", parts, [vmem] * len(parts), out, vmem, [], limit=VMEM // 4
    )


def passed_along(value, axis, steps):
    count = lax.axis_size(axis)
    pairs = [(source, (source + steps) % count) for source in range(count)]
    return lax.ppermute(value, axis, pairs)


def shards(intensities, object_field, probe_wave, owner_tile, row_offset, col_offset):
    tile_count = lax.axis_size("tile")
    slab_count = lax.axis_size("slab")
    extent = intensities.shape[1]
    depth, _, height, width = object_field.shape
    blocks = width // COLS
    tabs, kernel, permute = make_tables(extent)
    here = jnp.stack(
        [lax.axis_index("tile"), lax.axis_index("slab"), jnp.int32(slab_count)]
    ).astype(jnp.int32)
    own = jnp.transpose(
        object_field.reshape(depth, 2, height, blocks, COLS), (0, 1, 3, 2, 4)
    ).astype(bf16)
    tabs = jnp.stack(tabs)
    following = passed_along(own, "tile", -1)
    packed, meta = route(
        intensities, here, owner_tile, row_offset, col_offset,
        jnp.stack([permute, permute.T]), tile_count,
    )
    def gather(rows):
        return [rows] + [passed_along(rows, "slab", k) for k in range(1, slab_count)]

    mine0 = gather(own[0])
    packed, following, *mine0 = lax.optimization_barrier((packed, following, *mine0))
    images = lax.all_to_all(packed, "tile", split_axis=0, concat_axis=0, tiled=True)
    next0 = gather(following[0])
    second = gather(jnp.stack([own[1], following[1]]))
    first = mine0 + next0
    wave = waves(meta, first, probe_wave, kernel, tabs, slab_count)
    fields, total1, lower1 = misfits(meta, second, wave, images, tabs, slab_count)
    moved1 = passed_along(lower1, "tile", 1)
    mine1, *sends1 = combine(here, total1, moved1, slab_count)
    total0, lower0 = exits(meta, fields, probe_wave, kernel, tabs, blocks)
    lower0, mine1, *sends1 = lax.optimization_barrier((lower0, mine1, *sends1))
    moved0 = passed_along(lower0, "tile", 1)
    parts1 = [mine1] + [passed_along(x, "slab", k + 1) for k, x in enumerate(sends1)]
    mine0, *sends0 = combine(here, total0, moved0, slab_count)
    parts0 = [mine0] + [passed_along(x, "slab", k + 1) for k, x in enumerate(sends0)]
    return finish(parts0 + parts1, slab_count)


def solution(mesh):
    placed = (
        P(("tile", "slab"), None, None),
        P(None, None, ("tile", "slab"), None),
        P(),
        P(),
        P(),
        P(),
    )
    return jax.shard_map(
        shards,
        mesh=mesh,
        in_specs=placed,
        out_specs=P(None, None, ("tile", "slab"), None),
        check_vma=False,
    )
```

```python
import functools
import math

import jax
import jax.numpy as jnp
import ml_dtypes
import numpy as np
from jax import lax
from jax.experimental import pallas as pl
from jax.experimental.pallas import tpu as pltpu
from jax.sharding import PartitionSpec as P

K = 16
CAP = 2
GROUP = 4
WIDE = 8
CHUNK = 64
COLS = 128
chirp_strength = 40.0
bf16 = jnp.bfloat16
f32 = jnp.float32


def make_tables(extent):
    counter = np.arange(extent, dtype=np.int64)
    angles = (counter[:, None] * counter[None, :] % extent).astype(np.float32) * np.float32(
        2.0 * math.pi / extent
    )
    scaling = np.float32(1.0 / math.sqrt(extent))
    cosine = (np.cos(angles) * scaling).astype(ml_dtypes.bfloat16)
    sine_part = (np.sin(angles) * scaling).astype(ml_dtypes.bfloat16)
    half = extent // 2
    tables = []
    for parity in (0, 1):
        c, s = cosine[:half, parity::2], sine_part[:half, parity::2]
        table = np.concatenate([np.concatenate([c, -s], 1), np.concatenate([s, c], 1)], 0)
        tables += [table, np.ascontiguousarray(table.T)]
    order = np.concatenate([counter[0::2], counter[1::2]])
    frequency = (((counter + half) % extent - half).astype(np.float32) / extent)[order]
    phases = np.float32(chirp_strength) * (frequency[:, None] ** 2 + frequency[None, :] ** 2)
    kernel = np.stack([np.cos(phases), -np.sin(phases)]).astype(np.float32)
    permute = (counter[:, None] == order[None, :]).astype(ml_dtypes.bfloat16)
    return [jnp.asarray(t) for t in tables], jnp.asarray(kernel), jnp.asarray(permute)


def dot(a, b):
    return jnp.dot(a, b, preferred_element_type=f32)


def row_dot(fields, table):
    n = fields[0].shape[0]
    out = dot(jnp.concatenate(fields, 0), table)
    return [out[i * n : (i + 1) * n] for i in range(len(fields))]


def quads(a, b, h):
    return jnp.concatenate(
        [
            jnp.concatenate([a[:, :h], b[:, :h]], 1),
            jnp.concatenate([a[:, h:], b[:, h:]], 1),
        ],
        0,
    )


def folded(field):
    l, r = field
    return (
        jnp.concatenate([l[0] + r[0], l[1] + r[1]], 1).astype(bf16),
        jnp.concatenate([l[0] - r[0], l[1] - r[1]], 1).astype(bf16),
    )


def forward(items, tabs, narrow=False):
    a_even, t_even, a_odd, t_odd = tabs
    h = a_even.shape[0] // 2
    even = row_dot([x[0] for x in items], a_even)
    odd = row_dot([x[1] for x in items], a_odd)
    if narrow:
        even, odd = [x.astype(bf16) for x in even], [x.astype(bf16) for x in odd]
    plus = [quads(a[:h] + a[h:], b[:h] + b[h:], h).astype(bf16) for a, b in zip(even, odd)]
    minus = [quads(a[:h] - a[h:], b[:h] - b[h:], h).astype(bf16) for a, b in zip(even, odd)]
    return list(zip([dot(t_even, x) for x in plus], [dot(t_odd, x) for x in minus]))


def inverse(items, tabs, narrow=False):
    a_even, t_even, a_odd, t_odd = tabs
    h = a_even.shape[0] // 2

    def side(x, k):
        lanes = slice(k * h, (k + 1) * h)
        return jnp.concatenate(
            [jnp.concatenate([part[:h, lanes], part[h:, lanes]], 1) for part in x], 0
        )

    even = row_dot([side(x, 0) for x in items], t_even)
    odd = row_dot([side(x, 1) for x in items], t_odd)
    if narrow:
        even, odd = [x.astype(bf16) for x in even], [x.astype(bf16) for x in odd]
    plus = [a + b for a, b in zip(even, odd)]
    minus = [a - b for a, b in zip(even, odd)]
    low = [dot(a_even, quads(a[:h], b[:h], h).astype(bf16)) for a, b in zip(plus, minus)]
    high = [dot(a_odd, quads(a[h:], b[h:], h).astype(bf16)) for a, b in zip(plus, minus)]
    out = []
    for a, b in zip(low, high):
        s, d = a + b, a - b
        out.append(
            (jnp.concatenate([s[:h], d[:h]], 0), jnp.concatenate([s[h:], d[h:]], 0))
        )
    return out


def product(a, b):
    return a[0] * b[0] - a[1] * b[1], a[0] * b[1] + a[1] * b[0]


def product_conj(a, b):
    return a[0] * b[0] + a[1] * b[1], a[0] * b[1] - a[1] * b[0]


def cut(x):
    return x[0].astype(bf16), x[1].astype(bf16)


def halves(x, h=COLS):
    return (x[0][:, :h], x[1][:, :h]), (x[0][:, h:], x[1][:, h:])


def by_kernel(field, kernel_ref, conjugate):
    out = []
    h = field[0].shape[0] // 2
    op = product_conj if conjugate else product
    for k, part in enumerate(field):
        rows = slice(k * h, (k + 1) * h)
        spread = op((kernel_ref[0, rows, :], kernel_ref[1, rows, :]), (part[:h], part[h:]))
        out.append(jnp.concatenate(spread, 0).astype(bf16))
    return out


def window(rows_ref, top, col, extent):
    return tuple(
        tuple(rows_ref[plane, col + j, pl.ds(top, extent), :] for plane in (0, 1)) for j in (0, 1)
    )


def start_all(copies):
    for copy in copies:
        copy.start()
    return copies


def wait_all(copies):
    for copy in copies:
        copy.wait()


def copies_of(pairs, sems):
    return [pltpu.make_async_copy(a, b, sems.at[i]) for i, (a, b) in enumerate(pairs)]


def shard_copies(refs, shards):
    count = shards.shape[1]
    if len(refs) == count:
        return [(ref.at[side], shards.at[side, k]) for k, ref in enumerate(refs) for side in (0, 1)]
    return [(ref, shards.at[i // count, i % count]) for i, ref in enumerate(refs)]


def load_rows(slab_here, shards, rows_ref):
    count = shards.shape[1]
    height = shards.shape[-2]
    for side in (0, 1):
        for k in range(count):
            place = lax.rem(slab_here + count - k, count)
            start = pl.multiple_of((side * count + place) * height, height)
            rows_ref[:, :, pl.ds(start, height), :] = shards[side, k].astype(f32)


def group_count(meta_ref, size):
    return lax.div(meta_ref[4 * K] + size - 1, size)


def group_loop(meta_ref, ready, body, incoming=None, outgoing=None, size=GROUP):
    last = group_count(meta_ref, size)

    def each(make, group, do):
        if make is not None:
            for copy in make(group, lax.rem(group, 2)):
                do(copy)

    @pl.when(last > 0)
    def _():
        each(incoming, 0, lambda c: c.start())

    ready()

    def step(group, carry):
        @pl.when(group + 1 < last)
        def _():
            each(incoming, group + 1, lambda c: c.start())

        each(incoming, group, lambda c: c.wait())

        @pl.when(group >= 2)
        def _():
            each(outgoing, group - 2, lambda c: c.wait())

        body([size * group + j for j in range(size)], group, lax.rem(group, 2))
        each(outgoing, group, lambda c: c.start())
        return carry

    lax.fori_loop(0, last, step, 0)
    for back in (2, 1):

        @pl.when(last >= back)
        def _():
            each(outgoing, last - back, lambda c: c.wait())


def rows_of(field, start, count):
    return tuple(tuple(part[start : start + count] for part in side) for side in field)


def add_window(totals_ref, top, col, term, start=0):
    count = term[0][0].shape[0]
    for j in (0, 1):
        for plane in (0, 1):
            place = (plane, col + j, pl.ds(top + start, count), slice(None))
            totals_ref[place] += term[j][plane]


def route_kernel(
    here_ref, owner_hbm, row_hbm, col_hbm, images_hbm, permute_hbm, out_hbm, meta_ref,
    owner_ref, row_ref, col_ref, second_ref, images_ref, permute_ref, turned_ref, packed_ref,
    sems, in_sems, out_sems,
):
    reads, extent, _ = images_ref.shape
    tiles = out_hbm.shape[0] // CAP
    tile_here, slab_here, slabs = here_ref[0], here_ref[1], here_ref[2]
    mine = (tile_here * slabs + slab_here) * reads
    small = copies_of(
        [(owner_hbm, owner_ref), (row_hbm, row_ref), (col_hbm, col_ref), (permute_hbm, permute_ref)], sems
    )
    start_all(small)
    arriving = copies_of([(images_hbm.at[i], images_ref.at[i]) for i in range(reads)], in_sems)
    start_all(arriving)
    wait_all(small)
    owners = [owner_ref[mine + i] for i in range(reads)]
    leaving = []
    for group in (range(reads // 2), range(reads // 2, reads)):
        for i in group:
            arriving[i].wait()
        for i in group:
            turned_ref[i] = dot(images_ref[i], permute_ref[0]).astype(bf16)
        for i in group:
            packed_ref[i] = dot(permute_ref[1], turned_ref[i]).astype(bf16)
        for i in group:
            rank = jnp.int32(0)
            for j in range(i):
                rank += (owners[j] == owners[i]).astype(jnp.int32)
            copy = pltpu.make_async_copy(
                packed_ref.at[i], out_hbm.at[owners[i] * CAP + rank], out_sems.at[i]
            )
            copy.start()
            leaving.append(copy)

    def sender(g, counts):
        base = (g * slabs + slab_here) * reads
        first, later = counts
        seen = jnp.int32(0)
        for i in range(reads):
            match = (owner_ref[base + i] == tile_here).astype(jnp.int32)
            meta_ref[first] = base + i
            second_ref[later] = base + i
            fresh = match * (1 - seen)
            first, later, seen = first + fresh, later + match - fresh, seen + match
        return first, later

    first, later = lax.fori_loop(0, tiles, sender, (jnp.int32(0), jnp.int32(0)))
    total = first + later
    for i in range(K):
        in_first = i < first
        live = i < total
        row = jnp.where(in_first, meta_ref[i], second_ref[jnp.maximum(i - first, 0)])
        row = jnp.where(live, row, 0)
        group = row // (slabs * reads)
        meta_ref[i] = group * CAP + jnp.where(in_first, 0, 1)
        meta_ref[K + i] = row_ref[row]
        meta_ref[2 * K + i] = col_ref[row]
        meta_ref[3 * K + i] = jnp.where(live, row_ref[row], 2 * extent)
    meta_ref[4 * K] = total
    meta_ref[4 * K + 1] = first
    meta_ref[4 * K + 2] = slab_here
    wait_all(leaving)


def give_lower(totals_ref, lower_ref):
    rows = lower_ref.shape[2]
    lower_ref[...] = totals_ref[:, :, rows : 2 * rows, :].astype(bf16)


def combine_kernel(here_ref, own_ref, moved_ref, mine_ref, *send_refs):
    height = mine_ref.shape[2]
    count = len(send_refs) + 1
    for k in range(count):
        place = lax.rem(here_ref[1] + k, count)
        rows = pl.ds(pl.multiple_of(place * height, height), height)
        both = own_ref[:, :, rows, :] + moved_ref[:, :, rows, :].astype(f32)
        if k == 0:
            mine_ref[...] = both
        else:
            send_refs[k - 1][...] = both.astype(bf16)


def finish_kernel(count, *refs):
    out_ref = refs[-1]
    for s in range(out_ref.shape[0]):
        parts = refs[s * count : (s + 1) * count]
        for plane in (0, 1):
            for block in range(parts[0].shape[1]):
                total = parts[0][plane, block]
                for part in parts[1:]:
                    total = total + part[plane, block].astype(f32)
                out_ref[s, plane, :, block * COLS : (block + 1) * COLS] = total


def tables_of(tabs_ref):
    return tuple(tabs_ref[i] for i in range(4))


def wave_kernel(count, meta_ref, *refs):
    rows_hbm = refs[:count]
    (probe_hbm, kernel_hbm, tabs_hbm, wave_hbm,
     shards, probe_ref, kernel_ref, tabs, rows_ref, wave_buf, sems, out_sems) = refs[count:]
    extent = probe_ref.shape[0]
    once = start_all(copies_of(
        shard_copies(rows_hbm, shards)
        + [(probe_hbm, probe_ref), (kernel_hbm, kernel_ref), (tabs_hbm, tabs)], sems))

    def ready():
        wait_all(once)
        load_rows(meta_ref[4 * K + 2], shards, rows_ref)

    def outgoing(group, slot):
        return copies_of([(wave_buf.at[slot], wave_hbm.at[group])], out_sems.at[slot])

    def body(items, group, slot):
        tables = tables_of(tabs)
        probe = [cut(side) for side in halves((probe_ref[:, :extent], probe_ref[:, extent:]))]
        fields = []
        for at in items:
            w = window(rows_ref, meta_ref[K + at], meta_ref[2 * K + at], extent)
            fields.append(folded(tuple(product(p, cut(q)) for p, q in zip(probe, w))))
        spread = [by_kernel(x, kernel_ref, False) for x in forward(fields, tables, True)]
        for i, wave in enumerate(inverse(spread, tables, True)):
            wave_buf[slot, i, 0] = wave[0].astype(bf16)
            wave_buf[slot, i, 1] = wave[1].astype(bf16)

    group_loop(meta_ref, ready, body, None, outgoing)


def misfit_kernel(count, meta_ref, *refs):
    rows_hbm = refs[:count]
    (wave_hbm, images_hbm, tabs_hbm, back_ref, totals_ref, lower_ref,
     shards, tabs, rows_ref, wave_buf, image_buf, sems, in_sems) = refs[count:]
    extent = images_hbm.shape[1]
    h = extent // 2
    once = start_all(copies_of(shard_copies(rows_hbm, shards) + [(tabs_hbm, tabs)], sems))

    def ready():
        totals_ref[...] = jnp.zeros_like(totals_ref)
        wait_all(once)
        load_rows(meta_ref[4 * K + 2], shards, rows_ref)

    def incoming(group, slot):
        return copies_of(
            [(wave_hbm.at[group], wave_buf.at[slot])]
            + [(images_hbm.at[meta_ref[GROUP * group + i]], image_buf.at[slot, i]) for i in range(GROUP)],
            in_sems.at[slot],
        )

    def body(items, group, slot):
        tables = tables_of(tabs)

        def wave_of(i):
            return halves((wave_buf[slot, i, 0], wave_buf[slot, i, 1]))

        fields = []
        for i, at in enumerate(items):
            w = window(rows_ref, meta_ref[K + at], meta_ref[2 * K + at], extent)
            fields.append(folded(tuple(product(cut(p), cut(q)) for p, q in zip(wave_of(i), w))))
        far_grads = []
        for i, far in enumerate(forward(fields, tables, True)):
            parts = []
            for k, part in enumerate(far):
                re, im = part[:h], part[h:]
                image = image_buf[slot, i, k * h : (k + 1) * h, :].astype(f32)
                misfit = re * re + im * im - image
                parts.append(jnp.concatenate([re * misfit, im * misfit], 0).astype(bf16))
            far_grads.append(parts)
        for i, (at, grad) in enumerate(zip(items, inverse(far_grads, tables, True))):
            grad = halves(grad)
            top, col = meta_ref[K + at], meta_ref[2 * K + at]
            target = meta_ref[3 * K + at]
            for start in range(0, extent, CHUNK):
                rows = slice(start, start + CHUNK)
                part = rows_of(grad, start, CHUNK)
                wave = halves((wave_buf[slot, i, 0, rows].astype(f32), wave_buf[slot, i, 1, rows].astype(f32)))
                term = [product_conj(p, q) for p, q in zip(wave, part)]
                add_window(totals_ref, target, col, term, start)
                w = window(rows_ref, top + start, col, CHUNK)
                back = folded(tuple(product_conj(cut(p), cut(q)) for p, q in zip(w, part)))
                for k in (0, 1):
                    back_ref[at, k, rows] = back[k]

    group_loop(meta_ref, ready, body, incoming)
    give_lower(totals_ref, lower_ref)


def exit_kernel(
    meta_ref, fields_ref, probe_hbm, kernel_hbm, tabs_hbm, totals_ref, lower_ref, probe_ref, kernel_ref, tabs, sems
):
    extent = probe_ref.shape[0]
    once = start_all(copies_of([(probe_hbm, probe_ref), (kernel_hbm, kernel_ref), (tabs_hbm, tabs)], sems))

    def ready():
        totals_ref[...] = jnp.zeros_like(totals_ref)
        wait_all(once)

    def body(items, group, slot):
        tables = tables_of(tabs)
        fields = [(fields_ref[at, 0], fields_ref[at, 1]) for at in items]
        back = [by_kernel(x, kernel_ref, True) for x in forward(fields, tables)]
        grads = [halves(x) for x in inverse(back, tables)]
        for start in range(0, extent, CHUNK):
            rows = slice(start, start + CHUNK)
            probe = halves((probe_ref[rows, :extent], probe_ref[rows, extent:]))
            for at, grad in zip(items, grads):
                term = [product_conj(p, q) for p, q in zip(probe, rows_of(grad, start, CHUNK))]
                add_window(totals_ref, meta_ref[3 * K + at], meta_ref[2 * K + at], term, start)

    group_loop(meta_ref, ready, body, size=WIDE)
    give_lower(totals_ref, lower_ref)


MIB = 1024 * 1024
VMEM = 60 * MIB
LIMIT = 46 * MIB


smem = pl.BlockSpec(memory_space=pltpu.SMEM)
vmem = pl.BlockSpec(memory_space=pltpu.VMEM)
hbm = pl.BlockSpec(memory_space=pltpu.HBM)
anywhere = pl.BlockSpec(memory_space=pl.ANY)


def call(kernel, name, ins, in_specs, outs, out_specs, scratch, estimate=None, limit=VMEM):
    return pl.pallas_call(
        kernel,
        in_specs=in_specs,
        out_specs=out_specs,
        out_shape=outs,
        scratch_shapes=scratch,
        compiler_params=pltpu.CompilerParams(vmem_limit_bytes=limit),
        cost_estimate=estimate,
        name=name,
    )(*ins)


def cost(transforms, extent):
    return pl.CostEstimate(
        flops=int(K * transforms * 8 * 2 * extent**3), bytes_accessed=0, transcendentals=0
    )


def sems(*shape):
    return pltpu.SemaphoreType.DMA(shape)


def like(x):
    return pltpu.VMEM(x.shape, x.dtype)


def route(images, here, owner_tile, row_offset, col_offset, permute, tiles):
    reads, extent = images.shape[:2]
    outs = [
        pltpu.HBM((CAP * tiles, extent, extent), bf16),
        jax.ShapeDtypeStruct((4 * K + 8,), jnp.int32),
    ]
    numbers = pltpu.SMEM(owner_tile.shape, jnp.int32)
    scratch = [
        numbers, numbers, numbers, pltpu.SMEM((K + 8,), jnp.int32),
        like(images), like(permute), like(images), like(images), sems(4), sems(reads), sems(reads),
    ]
    ins = [here, owner_tile, row_offset, col_offset, images, permute]
    return call(route_kernel, "route", ins, [smem] + [hbm] * 5, outs, [hbm, smem], scratch, cost(0.25, extent))


def shards_scratch(rows, slabs):
    return pltpu.VMEM((2, slabs) + rows[0].shape[-4:], bf16)


def rows_padded(rows, slabs):
    planes, blocks, height, _ = rows[0].shape[-4:]
    return pltpu.VMEM((planes, blocks, 2 * slabs * height, COLS), f32)


def groups(extent, dtype):
    return pltpu.HBM((K // GROUP, GROUP, 2, extent, extent), dtype)


def group_buffer(extent, dtype):
    return pltpu.VMEM((2, GROUP, 2, extent, extent), dtype)


def waves(meta, rows, probe, kernel, tabs, slabs):
    extent = probe.shape[0]
    scratch = [
        shards_scratch(rows, slabs), like(probe), like(kernel), like(tabs), rows_padded(rows, slabs),
        group_buffer(extent, bf16), sems(2 * slabs + 3), sems(2, 1),
    ]
    return call(
        functools.partial(wave_kernel, len(rows)), "waves", [meta] + rows + [probe, kernel, tabs],
        [smem] + [anywhere] * len(rows) + [hbm] * 3, groups(extent, bf16), hbm, scratch,
        cost(2, extent),
    )


def totals_out(extent, blocks):
    return [
        pltpu.VMEM((2, blocks, 3 * extent, COLS), f32),
        jax.ShapeDtypeStruct((2, blocks, extent, COLS), bf16),
    ]


def misfits(meta, rows, wave, images, tabs, slabs):
    extent = images.shape[1]
    scratch = [
        shards_scratch(rows, slabs), like(tabs), rows_padded(rows, slabs),
        group_buffer(extent, bf16), pltpu.VMEM((2, GROUP, extent, extent), bf16),
        sems(2 * slabs + 1), sems(2, 1 + GROUP),
    ]
    return call(
        functools.partial(misfit_kernel, len(rows)), "misfits", [meta] + rows + [wave, images, tabs],
        [smem] + [anywhere] * len(rows) + [hbm, anywhere, hbm],
        [pltpu.VMEM((K, 2, extent, extent), bf16)] + totals_out(extent, rows[0].shape[-3]), [vmem, vmem, vmem],
        scratch, cost(2, extent), limit=LIMIT,
    )


def exits(meta, fields, probe, kernel, tabs, blocks):
    extent = probe.shape[0]
    return call(
        exit_kernel, "exits", [meta, fields, probe, kernel, tabs], [smem, vmem, hbm, hbm, hbm],
        totals_out(extent, blocks), [vmem, vmem], [like(probe), like(kernel), like(tabs), sems(3)],
        cost(0.1, extent), limit=30 * MIB,
    )


def combine(here, own, moved, count):
    shape = own.shape[:2] + (moved.shape[2] // count, COLS)
    outs = [jax.ShapeDtypeStruct(shape, f32 if k == 0 else bf16) for k in range(count)]
    return call(combine_kernel, "combine", [here, own, moved], [smem, vmem, vmem], outs, [vmem] * count, [], limit=VMEM // 4)


def finish(parts, count):
    blocks, height = parts[0].shape[1:3]
    out = jax.ShapeDtypeStruct((len(parts) // count, 2, height, blocks * COLS), f32)
    return call(
        functools.partial(finish_kernel, count), "finish", parts, [vmem] * len(parts), out, vmem, [], limit=VMEM // 4
    )


def passed_along(value, axis, steps):
    count = lax.axis_size(axis)
    pairs = [(source, (source + steps) % count) for source in range(count)]
    return lax.ppermute(value, axis, pairs)


def shards(intensities, object_field, probe_wave, owner_tile, row_offset, col_offset):
    tile_count = lax.axis_size("tile")
    slab_count = lax.axis_size("slab")
    extent = intensities.shape[1]
    depth, _, height, width = object_field.shape
    blocks = width // COLS
    tabs, kernel, permute = make_tables(extent)
    here = jnp.stack(
        [lax.axis_index("tile"), lax.axis_index("slab"), jnp.int32(slab_count)]
    ).astype(jnp.int32)
    own = jnp.transpose(
        object_field.reshape(depth, 2, height, blocks, COLS), (0, 1, 3, 2, 4)
    ).astype(bf16)
    tabs = jnp.stack(tabs)
    following = passed_along(own, "tile", -1)
    packed, meta = route(
        intensities, here, owner_tile, row_offset, col_offset,
        jnp.stack([permute, permute.T]), tile_count,
    )
    def gather(rows):
        return [rows] + [passed_along(rows, "slab", k) for k in range(1, slab_count)]

    mine0 = gather(own[0])
    packed, following, *mine0 = lax.optimization_barrier((packed, following, *mine0))
    images = lax.all_to_all(packed, "tile", split_axis=0, concat_axis=0, tiled=True)
    next0 = gather(following[0])
    second = gather(jnp.stack([own[1], following[1]]))
    first = mine0 + next0
    wave = waves(meta, first, probe_wave, kernel, tabs, slab_count)
    fields, total1, lower1 = misfits(meta, second, wave, images, tabs, slab_count)
    moved1 = passed_along(lower1, "tile", 1)
    mine1, *sends1 = combine(here, total1, moved1, slab_count)
    total0, lower0 = exits(meta, fields, probe_wave, kernel, tabs, blocks)
    lower0, mine1, *sends1 = lax.optimization_barrier((lower0, mine1, *sends1))
    moved0 = passed_along(lower0, "tile", 1)
    parts1 = [mine1] + [passed_along(x, "slab", k + 1) for k, x in enumerate(sends1)]
    mine0, *sends0 = combine(here, total0, moved0, slab_count)
    parts0 = [mine0] + [passed_along(x, "slab", k + 1) for k, x in enumerate(sends0)]
    return finish(parts0 + parts1, slab_count)


def solution(mesh):
    placed = (
        P(("tile", "slab"), None, None),
        P(None, None, ("tile", "slab"), None),
        P(),
        P(),
        P(),
        P(),
    )
    return jax.shard_map(
        shards,
        mesh=mesh,
        in_specs=placed,
        out_specs=P(None, None, ("tile", "slab"), None),
        check_vma=False,
    )
```

```python
import functools
import math

import jax
import jax.numpy as jnp
import ml_dtypes
import numpy as np
from jax import lax
from jax.experimental import pallas as pl
from jax.experimental.pallas import tpu as pltpu
from jax.sharding import PartitionSpec as P

K = 16
CAP = 2
GROUP = 4
WIDE = 8
CHUNK = 64
COLS = 128
chirp_strength = 40.0
bf16 = jnp.bfloat16
f32 = jnp.float32


def make_tables(extent):
    counter = np.arange(extent, dtype=np.int64)
    angles = (counter[:, None] * counter[None, :] % extent).astype(np.float32) * np.float32(
        2.0 * math.pi / extent
    )
    scaling = np.float32(1.0 / math.sqrt(extent))
    cosine = (np.cos(angles) * scaling).astype(ml_dtypes.bfloat16)
    sine_part = (np.sin(angles) * scaling).astype(ml_dtypes.bfloat16)
    half = extent // 2
    tables = []
    for parity in (0, 1):
        c, s = cosine[:half, parity::2], sine_part[:half, parity::2]
        table = np.concatenate([np.concatenate([c, -s], 1), np.concatenate([s, c], 1)], 0)
        tables += [table, np.ascontiguousarray(table.T)]
    order = np.concatenate([counter[0::2], counter[1::2]])
    frequency = (((counter + half) % extent - half).astype(np.float32) / extent)[order]
    phases = np.float32(chirp_strength) * (frequency[:, None] ** 2 + frequency[None, :] ** 2)
    kernel = np.stack([np.cos(phases), -np.sin(phases)]).astype(np.float32)
    permute = (counter[:, None] == order[None, :]).astype(ml_dtypes.bfloat16)
    return [jnp.asarray(t) for t in tables], jnp.asarray(kernel), jnp.asarray(permute)


def dot(a, b):
    return jnp.dot(a, b, preferred_element_type=f32)


def row_dot(fields, table):
    n = fields[0].shape[0]
    out = dot(jnp.concatenate(fields, 0), table)
    return [out[i * n : (i + 1) * n] for i in range(len(fields))]


def quads(a, b, h):
    return jnp.concatenate(
        [
            jnp.concatenate([a[:, :h], b[:, :h]], 1),
            jnp.concatenate([a[:, h:], b[:, h:]], 1),
        ],
        0,
    )


def folded(field):
    l, r = field
    return (
        jnp.concatenate([l[0] + r[0], l[1] + r[1]], 1).astype(bf16),
        jnp.concatenate([l[0] - r[0], l[1] - r[1]], 1).astype(bf16),
    )


def forward(items, tabs, narrow=False):
    a_even, t_even, a_odd, t_odd = tabs
    h = a_even.shape[0] // 2
    even = row_dot([x[0] for x in items], a_even)
    odd = row_dot([x[1] for x in items], a_odd)
    if narrow:
        even, odd = [x.astype(bf16) for x in even], [x.astype(bf16) for x in odd]
    plus = [quads(a[:h] + a[h:], b[:h] + b[h:], h).astype(bf16) for a, b in zip(even, odd)]
    minus = [quads(a[:h] - a[h:], b[:h] - b[h:], h).astype(bf16) for a, b in zip(even, odd)]
    return list(zip([dot(t_even, x) for x in plus], [dot(t_odd, x) for x in minus]))


def inverse(items, tabs, narrow=False):
    a_even, t_even, a_odd, t_odd = tabs
    h = a_even.shape[0] // 2

    def side(x, k):
        lanes = slice(k * h, (k + 1) * h)
        return jnp.concatenate(
            [jnp.concatenate([part[:h, lanes], part[h:, lanes]], 1) for part in x], 0
        )

    even = row_dot([side(x, 0) for x in items], t_even)
    odd = row_dot([side(x, 1) for x in items], t_odd)
    if narrow:
        even, odd = [x.astype(bf16) for x in even], [x.astype(bf16) for x in odd]
    plus = [a + b for a, b in zip(even, odd)]
    minus = [a - b for a, b in zip(even, odd)]
    low = [dot(a_even, quads(a[:h], b[:h], h).astype(bf16)) for a, b in zip(plus, minus)]
    high = [dot(a_odd, quads(a[h:], b[h:], h).astype(bf16)) for a, b in zip(plus, minus)]
    out = []
    for a, b in zip(low, high):
        s, d = a + b, a - b
        out.append(
            (jnp.concatenate([s[:h], d[:h]], 0), jnp.concatenate([s[h:], d[h:]], 0))
        )
    return out


def product(a, b):
    return a[0] * b[0] - a[1] * b[1], a[0] * b[1] + a[1] * b[0]


def product_conj(a, b):
    return a[0] * b[0] + a[1] * b[1], a[0] * b[1] - a[1] * b[0]


def cut(x):
    return x[0].astype(bf16), x[1].astype(bf16)


def halves(x, h=COLS):
    return (x[0][:, :h], x[1][:, :h]), (x[0][:, h:], x[1][:, h:])


def by_kernel(field, kernel_ref, conjugate):
    out = []
    h = field[0].shape[0] // 2
    op = product_conj if conjugate else product
    for k, part in enumerate(field):
        rows = slice(k * h, (k + 1) * h)
        spread = op((kernel_ref[0, rows, :], kernel_ref[1, rows, :]), (part[:h], part[h:]))
        out.append(jnp.concatenate(spread, 0).astype(bf16))
    return out


def window(rows_ref, top, col, extent):
    return tuple(
        tuple(rows_ref[plane, col + j, pl.ds(top, extent), :] for plane in (0, 1)) for j in (0, 1)
    )


def start_all(copies):
    for copy in copies:
        copy.start()
    return copies


def wait_all(copies):
    for copy in copies:
        copy.wait()


def copies_of(pairs, sems):
    return [pltpu.make_async_copy(a, b, sems.at[i]) for i, (a, b) in enumerate(pairs)]


def shard_copies(refs, shards):
    count = shards.shape[1]
    if len(refs) == count:
        return [(ref.at[side], shards.at[side, k]) for k, ref in enumerate(refs) for side in (0, 1)]
    return [(ref, shards.at[i // count, i % count]) for i, ref in enumerate(refs)]


def load_rows(slab_here, shards, rows_ref):
    count = shards.shape[1]
    height = shards.shape[-2]
    for side in (0, 1):
        for k in range(count):
            place = lax.rem(slab_here + count - k, count)
            start = pl.multiple_of((side * count + place) * height, height)
            rows_ref[:, :, pl.ds(start, height), :] = shards[side, k].astype(f32)


def group_count(meta_ref, size):
    return lax.div(meta_ref[4 * K] + size - 1, size)


def group_loop(meta_ref, ready, body, incoming=None, outgoing=None, size=GROUP):
    last = group_count(meta_ref, size)

    def each(make, group, do):
        if make is not None:
            for copy in make(group, lax.rem(group, 2)):
                do(copy)

    @pl.when(last > 0)
    def _():
        each(incoming, 0, lambda c: c.start())

    ready()

    def step(group, carry):
        @pl.when(group + 1 < last)
        def _():
            each(incoming, group + 1, lambda c: c.start())

        each(incoming, group, lambda c: c.wait())

        @pl.when(group >= 2)
        def _():
            each(outgoing, group - 2, lambda c: c.wait())

        body([size * group + j for j in range(size)], group, lax.rem(group, 2))
        each(outgoing, group, lambda c: c.start())
        return carry

    lax.fori_loop(0, last, step, 0)
    for back in (2, 1):

        @pl.when(last >= back)
        def _():
            each(outgoing, last - back, lambda c: c.wait())


def rows_of(field, start, count):
    return tuple(tuple(part[start : start + count] for part in side) for side in field)


def add_window(totals_ref, top, col, term, start=0):
    count = term[0][0].shape[0]
    for j in (0, 1):
        for plane in (0, 1):
            place = (plane, col + j, pl.ds(top + start, count), slice(None))
            totals_ref[place] += term[j][plane].astype(f32)


def route_kernel(
    here_ref, owner_hbm, row_hbm, col_hbm, images_hbm, permute_hbm, out_hbm, meta_ref,
    owner_ref, row_ref, col_ref, second_ref, images_ref, permute_ref, turned_ref, packed_ref,
    sems, in_sems, out_sems,
):
    reads, extent, _ = images_ref.shape
    tiles = out_hbm.shape[0] // CAP
    tile_here, slab_here, slabs = here_ref[0], here_ref[1], here_ref[2]
    mine = (tile_here * slabs + slab_here) * reads
    small = copies_of(
        [(owner_hbm, owner_ref), (row_hbm, row_ref), (col_hbm, col_ref), (permute_hbm, permute_ref)], sems
    )
    start_all(small)
    arriving = copies_of([(images_hbm.at[i], images_ref.at[i]) for i in range(reads)], in_sems)
    start_all(arriving)
    wait_all(small)
    owners = [owner_ref[mine + i] for i in range(reads)]
    leaving = []
    for group in (range(reads // 2), range(reads // 2, reads)):
        for i in group:
            arriving[i].wait()
        for i in group:
            turned_ref[i] = dot(images_ref[i], permute_ref[0]).astype(bf16)
        for i in group:
            packed_ref[i] = dot(permute_ref[1], turned_ref[i]).astype(bf16)
        for i in group:
            rank = jnp.int32(0)
            for j in range(i):
                rank += (owners[j] == owners[i]).astype(jnp.int32)
            copy = pltpu.make_async_copy(
                packed_ref.at[i], out_hbm.at[owners[i] * CAP + rank], out_sems.at[i]
            )
            copy.start()
            leaving.append(copy)

    def sender(g, counts):
        base = (g * slabs + slab_here) * reads
        first, later = counts
        seen = jnp.int32(0)
        for i in range(reads):
            match = (owner_ref[base + i] == tile_here).astype(jnp.int32)
            meta_ref[first] = base + i
            second_ref[later] = base + i
            fresh = match * (1 - seen)
            first, later, seen = first + fresh, later + match - fresh, seen + match
        return first, later

    first, later = lax.fori_loop(0, tiles, sender, (jnp.int32(0), jnp.int32(0)))
    total = first + later
    for i in range(K):
        in_first = i < first
        live = i < total
        row = jnp.where(in_first, meta_ref[i], second_ref[jnp.maximum(i - first, 0)])
        row = jnp.where(live, row, 0)
        group = row // (slabs * reads)
        meta_ref[i] = group * CAP + jnp.where(in_first, 0, 1)
        meta_ref[K + i] = row_ref[row]
        meta_ref[2 * K + i] = col_ref[row]
        meta_ref[3 * K + i] = jnp.where(live, row_ref[row], 2 * extent)
    meta_ref[4 * K] = total
    meta_ref[4 * K + 1] = first
    meta_ref[4 * K + 2] = slab_here
    wait_all(leaving)


def give_lower(totals_ref, lower_ref):
    rows = lower_ref.shape[2]
    lower_ref[...] = totals_ref[:, :, rows : 2 * rows, :].astype(bf16)


def combine_kernel(here_ref, own_ref, moved_ref, mine_ref, *send_refs):
    height = mine_ref.shape[2]
    count = len(send_refs) + 1
    for k in range(count):
        place = lax.rem(here_ref[1] + k, count)
        rows = pl.ds(pl.multiple_of(place * height, height), height)
        both = own_ref[:, :, rows, :] + moved_ref[:, :, rows, :].astype(f32)
        if k == 0:
            mine_ref[...] = both
        else:
            send_refs[k - 1][...] = both.astype(bf16)


def finish_kernel(count, *refs):
    out_ref = refs[-1]
    for s in range(out_ref.shape[0]):
        parts = refs[s * count : (s + 1) * count]
        for plane in (0, 1):
            for block in range(parts[0].shape[1]):
                total = parts[0][plane, block]
                for part in parts[1:]:
                    total = total + part[plane, block].astype(f32)
                out_ref[s, plane, :, block * COLS : (block + 1) * COLS] = total


def tables_of(tabs_ref):
    return tuple(tabs_ref[i] for i in range(4))


def wave_kernel(count, meta_ref, *refs):
    rows_hbm = refs[:count]
    (probe_hbm, kernel_hbm, tabs_hbm, wave_hbm,
     shards, probe_ref, kernel_ref, tabs, rows_ref, wave_buf, sems, out_sems) = refs[count:]
    extent = probe_ref.shape[0]
    once = start_all(copies_of(
        shard_copies(rows_hbm, shards)
        + [(probe_hbm, probe_ref), (kernel_hbm, kernel_ref), (tabs_hbm, tabs)], sems))

    def ready():
        wait_all(once)
        load_rows(meta_ref[4 * K + 2], shards, rows_ref)

    def outgoing(group, slot):
        return copies_of([(wave_buf.at[slot], wave_hbm.at[group])], out_sems.at[slot])

    def body(items, group, slot):
        tables = tables_of(tabs)
        probe = [cut(side) for side in halves((probe_ref[:, :extent], probe_ref[:, extent:]))]
        fields = []
        for at in items:
            w = window(rows_ref, meta_ref[K + at], meta_ref[2 * K + at], extent)
            fields.append(folded(tuple(product(p, cut(q)) for p, q in zip(probe, w))))
        spread = [by_kernel(x, kernel_ref, False) for x in forward(fields, tables, True)]
        for i, wave in enumerate(inverse(spread, tables, True)):
            wave_buf[slot, i, 0] = wave[0].astype(bf16)
            wave_buf[slot, i, 1] = wave[1].astype(bf16)

    group_loop(meta_ref, ready, body, None, outgoing)


def misfit_kernel(count, meta_ref, *refs):
    rows_hbm = refs[:count]
    (wave_hbm, images_hbm, tabs_hbm, back_ref, totals_ref, lower_ref,
     shards, tabs, rows_ref, wave_buf, image_buf, sems, in_sems) = refs[count:]
    extent = images_hbm.shape[1]
    h = extent // 2
    once = start_all(copies_of(shard_copies(rows_hbm, shards) + [(tabs_hbm, tabs)], sems))

    def ready():
        totals_ref[...] = jnp.zeros_like(totals_ref)
        wait_all(once)
        load_rows(meta_ref[4 * K + 2], shards, rows_ref)

    def incoming(group, slot):
        return copies_of(
            [(wave_hbm.at[group], wave_buf.at[slot])]
            + [(images_hbm.at[meta_ref[GROUP * group + i]], image_buf.at[slot, i]) for i in range(GROUP)],
            in_sems.at[slot],
        )

    def body(items, group, slot):
        tables = tables_of(tabs)

        def wave_of(i):
            return halves((wave_buf[slot, i, 0], wave_buf[slot, i, 1]))

        fields = []
        for i, at in enumerate(items):
            w = window(rows_ref, meta_ref[K + at], meta_ref[2 * K + at], extent)
            fields.append(folded(tuple(product(cut(p), cut(q)) for p, q in zip(wave_of(i), w))))
        far_grads = []
        for i, far in enumerate(forward(fields, tables, True)):
            parts = []
            for k, part in enumerate(far):
                re, im = part[:h], part[h:]
                image = image_buf[slot, i, k * h : (k + 1) * h, :].astype(f32)
                misfit = re * re + im * im - image
                parts.append(jnp.concatenate([re * misfit, im * misfit], 0).astype(bf16))
            far_grads.append(parts)
        for i, (at, grad) in enumerate(zip(items, inverse(far_grads, tables, True))):
            grad = halves(grad)
            top, col = meta_ref[K + at], meta_ref[2 * K + at]
            target = meta_ref[3 * K + at]
            for start in range(0, extent, CHUNK):
                rows = slice(start, start + CHUNK)
                part = rows_of(grad, start, CHUNK)
                wave = halves((wave_buf[slot, i, 0, rows], wave_buf[slot, i, 1, rows]))
                short = [cut(side) for side in part]
                term = [product_conj(p, q) for p, q in zip(wave, short)]
                add_window(totals_ref, target, col, term, start)
                w = window(rows_ref, top + start, col, CHUNK)
                back = folded(tuple(product_conj(cut(p), q) for p, q in zip(w, short)))
                for k in (0, 1):
                    back_ref[at, k, rows] = back[k]

    group_loop(meta_ref, ready, body, incoming)
    give_lower(totals_ref, lower_ref)


def exit_kernel(
    meta_ref, fields_ref, probe_hbm, kernel_hbm, tabs_hbm, totals_ref, lower_ref, probe_ref, kernel_ref, tabs, sems
):
    extent = probe_ref.shape[0]
    once = start_all(copies_of([(probe_hbm, probe_ref), (kernel_hbm, kernel_ref), (tabs_hbm, tabs)], sems))

    def ready():
        totals_ref[...] = jnp.zeros_like(totals_ref)
        wait_all(once)

    def body(items, group, slot):
        tables = tables_of(tabs)
        fields = [(fields_ref[at, 0], fields_ref[at, 1]) for at in items]
        back = [by_kernel(x, kernel_ref, True) for x in forward(fields, tables)]
        grads = [halves(x) for x in inverse(back, tables)]
        for start in range(0, extent, CHUNK):
            rows = slice(start, start + CHUNK)
            probe = halves((probe_ref[rows, :extent], probe_ref[rows, extent:]))
            for at, grad in zip(items, grads):
                term = [product_conj(p, q) for p, q in zip(probe, rows_of(grad, start, CHUNK))]
                add_window(totals_ref, meta_ref[3 * K + at], meta_ref[2 * K + at], term, start)

    group_loop(meta_ref, ready, body, size=WIDE)
    give_lower(totals_ref, lower_ref)


MIB = 1024 * 1024
VMEM = 60 * MIB
LIMIT = 46 * MIB


smem = pl.BlockSpec(memory_space=pltpu.SMEM)
vmem = pl.BlockSpec(memory_space=pltpu.VMEM)
hbm = pl.BlockSpec(memory_space=pltpu.HBM)
anywhere = pl.BlockSpec(memory_space=pl.ANY)


def call(kernel, name, ins, in_specs, outs, out_specs, scratch, estimate=None, limit=VMEM):
    return pl.pallas_call(
        kernel,
        in_specs=in_specs,
        out_specs=out_specs,
        out_shape=outs,
        scratch_shapes=scratch,
        compiler_params=pltpu.CompilerParams(vmem_limit_bytes=limit),
        cost_estimate=estimate,
        name=name,
    )(*ins)


def cost(transforms, extent):
    return pl.CostEstimate(
        flops=int(K * transforms * 8 * 2 * extent**3), bytes_accessed=0, transcendentals=0
    )


def sems(*shape):
    return pltpu.SemaphoreType.DMA(shape)


def like(x):
    return pltpu.VMEM(x.shape, x.dtype)


def route(images, here, owner_tile, row_offset, col_offset, permute, tiles):
    reads, extent = images.shape[:2]
    outs = [
        pltpu.HBM((CAP * tiles, extent, extent), bf16),
        jax.ShapeDtypeStruct((4 * K + 8,), jnp.int32),
    ]
    numbers = pltpu.SMEM(owner_tile.shape, jnp.int32)
    scratch = [
        numbers, numbers, numbers, pltpu.SMEM((K + 8,), jnp.int32),
        like(images), like(permute), like(images), like(images), sems(4), sems(reads), sems(reads),
    ]
    ins = [here, owner_tile, row_offset, col_offset, images, permute]
    return call(route_kernel, "route", ins, [smem] + [hbm] * 5, outs, [hbm, smem], scratch, cost(0.25, extent))


def shards_scratch(rows, slabs):
    return pltpu.VMEM((2, slabs) + rows[0].shape[-4:], bf16)


def rows_padded(rows, slabs):
    planes, blocks, height, _ = rows[0].shape[-4:]
    return pltpu.VMEM((planes, blocks, 2 * slabs * height, COLS), f32)


def groups(extent, dtype):
    return pltpu.HBM((K // GROUP, GROUP, 2, extent, extent), dtype)


def group_buffer(extent, dtype):
    return pltpu.VMEM((2, GROUP, 2, extent, extent), dtype)


def waves(meta, rows, probe, kernel, tabs, slabs):
    extent = probe.shape[0]
    scratch = [
        shards_scratch(rows, slabs), like(probe), like(kernel), like(tabs), rows_padded(rows, slabs),
        group_buffer(extent, bf16), sems(2 * slabs + 3), sems(2, 1),
    ]
    return call(
        functools.partial(wave_kernel, len(rows)), "waves", [meta] + rows + [probe, kernel, tabs],
        [smem] + [anywhere] * len(rows) + [hbm] * 3, groups(extent, bf16), hbm, scratch,
        cost(2, extent),
    )


def totals_out(extent, blocks):
    return [
        pltpu.VMEM((2, blocks, 3 * extent, COLS), f32),
        jax.ShapeDtypeStruct((2, blocks, extent, COLS), bf16),
    ]


def misfits(meta, rows, wave, images, tabs, slabs):
    extent = images.shape[1]
    scratch = [
        shards_scratch(rows, slabs), like(tabs), rows_padded(rows, slabs),
        group_buffer(extent, bf16), pltpu.VMEM((2, GROUP, extent, extent), bf16),
        sems(2 * slabs + 1), sems(2, 1 + GROUP),
    ]
    return call(
        functools.partial(misfit_kernel, len(rows)), "misfits", [meta] + rows + [wave, images, tabs],
        [smem] + [anywhere] * len(rows) + [hbm, anywhere, hbm],
        [pltpu.VMEM((K, 2, extent, extent), bf16)] + totals_out(extent, rows[0].shape[-3]), [vmem, vmem, vmem],
        scratch, cost(2, extent), limit=LIMIT,
    )


def exits(meta, fields, probe, kernel, tabs, blocks):
    extent = probe.shape[0]
    return call(
        exit_kernel, "exits", [meta, fields, probe, kernel, tabs], [smem, vmem, hbm, hbm, hbm],
        totals_out(extent, blocks), [vmem, vmem], [like(probe), like(kernel), like(tabs), sems(3)],
        cost(0.1, extent), limit=30 * MIB,
    )


def combine(here, own, moved, count):
    shape = own.shape[:2] + (moved.shape[2] // count, COLS)
    outs = [jax.ShapeDtypeStruct(shape, f32 if k == 0 else bf16) for k in range(count)]
    return call(combine_kernel, "combine", [here, own, moved], [smem, vmem, vmem], outs, [vmem] * count, [], limit=VMEM // 4)


def finish(parts, count):
    blocks, height = parts[0].shape[1:3]
    out = jax.ShapeDtypeStruct((len(parts) // count, 2, height, blocks * COLS), f32)
    return call(
        functools.partial(finish_kernel, count), "finish", parts, [vmem] * len(parts), out, vmem, [], limit=VMEM // 4
    )


def passed_along(value, axis, steps):
    count = lax.axis_size(axis)
    pairs = [(source, (source + steps) % count) for source in range(count)]
    return lax.ppermute(value, axis, pairs)


def shards(intensities, object_field, probe_wave, owner_tile, row_offset, col_offset):
    tile_count = lax.axis_size("tile")
    slab_count = lax.axis_size("slab")
    extent = intensities.shape[1]
    depth, _, height, width = object_field.shape
    blocks = width // COLS
    tabs, kernel, permute = make_tables(extent)
    here = jnp.stack(
        [lax.axis_index("tile"), lax.axis_index("slab"), jnp.int32(slab_count)]
    ).astype(jnp.int32)
    own = jnp.transpose(
        object_field.reshape(depth, 2, height, blocks, COLS), (0, 1, 3, 2, 4)
    ).astype(bf16)
    tabs = jnp.stack(tabs)
    following = passed_along(own, "tile", -1)
    packed, meta = route(
        intensities, here, owner_tile, row_offset, col_offset,
        jnp.stack([permute, permute.T]), tile_count,
    )
    def gather(rows):
        return [rows] + [passed_along(rows, "slab", k) for k in range(1, slab_count)]

    mine0 = gather(own[0])
    packed, following, *mine0 = lax.optimization_barrier((packed, following, *mine0))
    images = lax.all_to_all(packed, "tile", split_axis=0, concat_axis=0, tiled=True)
    next0 = gather(following[0])
    second = gather(jnp.stack([own[1], following[1]]))
    first = mine0 + next0
    wave = waves(meta, first, probe_wave, kernel, tabs, slab_count)
    fields, total1, lower1 = misfits(meta, second, wave, images, tabs, slab_count)
    moved1 = passed_along(lower1, "tile", 1)
    mine1, *sends1 = combine(here, total1, moved1, slab_count)
    total0, lower0 = exits(meta, fields, probe_wave, kernel, tabs, blocks)
    lower0, mine1, *sends1 = lax.optimization_barrier((lower0, mine1, *sends1))
    moved0 = passed_along(lower0, "tile", 1)
    parts1 = [mine1] + [passed_along(x, "slab", k + 1) for k, x in enumerate(sends1)]
    mine0, *sends0 = combine(here, total0, moved0, slab_count)
    parts0 = [mine0] + [passed_along(x, "slab", k + 1) for k, x in enumerate(sends0)]
    return finish(parts0 + parts1, slab_count)


def solution(mesh):
    placed = (
        P(("tile", "slab"), None, None),
        P(None, None, ("tile", "slab"), None),
        P(),
        P(),
        P(),
        P(),
    )
    return jax.shard_map(
        shards,
        mesh=mesh,
        in_specs=placed,
        out_specs=P(None, None, ("tile", "slab"), None),
        check_vma=False,
    )
```
